128 devices in a mesh: rec: 4 (over y), tm: 32 (over z, x, core).
Axes of the slice: x: 4, y: 4, z: 4, core: 2. Of those that a mesh axis runs over, the one named last changes fastest.
Arguments:
- frames: bfloat16 [4, 12288, 768], P('rec', 'tm'), may hold values from -6 to 6
- cotangent: bfloat16 [4, 12288, 768], P('rec', 'tm'), may hold values from -6 to 6
- routes: int32 [4, 12288, 1], P('rec', 'tm'), may hold values from 0 to 127; in each aligned block of 384 rows (0 to 383, 384 to 767, ..., all dimensions but the last counted through in order) at most 4 rows name the same one
- lengths: int32 [4], P('rec'), may hold values from 3072 to 12288, as said below
- conv_weight: float32 [31, 768], replicated, may hold values from -0.875 to 0.875
- norm_gain: float32 [768], replicated, may hold values from 0.25 to 1.75
- expert_in: bfloat16 [128, 768, 3072], P(('rec', 'tm')), may hold values from -0.21875 to 0.21875
- expert_out: bfloat16 [128, 3072, 768], P(('rec', 'tm')), may hold values from -0.109375 to 0.109375
Outputs:
- output: bfloat16 [4, 12288, 768], P('rec', 'tm')
- grad_frames: bfloat16 [4, 12288, 768], P('rec', 'tm')
- grad_conv: float32 [31, 768], replicated
- grad_gain: float32 [768], replicated
- grad_in: bfloat16 [128, 768, 3072], P(('rec', 'tm'))
- grad_out: bfloat16 [128, 3072, 768], P(('rec', 'tm'))
The draws below stay inside these ranges and needn't reach their ends.
Inputs may be any that keep to these rules, and one draw needn't show every extreme that they name: `routes`: in the rows of one device no expert is named by more than 4 frames. `lengths`: some recording has all 12288 frames valid and another has exactly 3072.
All inputs are finite; a program needn't handle non-finite values.
Results may differ from the reference program's by a relative error of at most 0.006.
Values may be sent and summed in bfloat16 or wider, within the bound.
No kernel may reach another device: no remote copies, remote signals or barrier semaphores. Data moves between devices by JAX's collectives and lax.ppermute only.
A program may use at most 128 MiB of HBM per device.

```python
import math
import jax
import jax.numpy as jnp
import numpy as np
from jax import lax

D = 768
H = 3072
KERNEL = 31
FR_DEV = 384
REC = 4
FRAMES = 12288
EXPERTS = 128
CAP = 4


def draw_lengths(key, part):
    key = jax.random.fold_in(key, 11)
    first_key, second_key = jax.random.split(key)
    random_lens = jax.random.randint(first_key, (REC,), FRAMES // 4, FRAMES + 1)
    chosen = jax.random.randint(second_key, (), 0, REC)
    shortest = (chosen + 1) % REC
    positions = jnp.arange(REC)
    picked = jnp.where(positions == shortest, FRAMES // 4, random_lens)
    return jnp.where(positions == chosen, FRAMES, picked).astype(jnp.int32)


def steps_of(key, shape, pieces, low, high):
    def one(position, shards_of):
        draws = jax.random.uniform(jax.random.fold_in(jax.random.fold_in(key, 6), position), (shards_of,), jnp.float32, low / len(pieces), high / len(pieces))
        return jnp.repeat(jnp.exp(draws), shape[position] // shards_of).reshape((-1,) + (1,) * (len(shape) - position - 1))

    loudness = one(*pieces[0])
    for cut in pieces[1:]:
        loudness = loudness * one(*cut)
    return loudness


def assign_block(key, own, number, rows, amount, top, limit, slope):
    order = jax.random.permutation(key, amount)
    packed, common = shares(amount, rows * top, limit, slope, True), shares(amount, rows * top, limit, slope, False)
    places = jnp.arange(amount)

    def named(tallies, rotation):
        used = int((tallies > 0).sum())
        fixed = max(1, used // 4)
        shifted = fixed + (places - fixed + rotation * (used - fixed)) % max(1, amount - fixed)
        return jnp.zeros((amount,), jnp.int32).at[order[jnp.where(places < fixed, places, shifted)]].set(jnp.asarray(tallies, jnp.int32))

    tallies = jnp.where(number % 4 == 0, named(packed, number // 4), named(common, number - number // 4 - 1))
    mixed = jax.random.permutation(jax.random.fold_in(own, 3), amount)
    donor, sink = mixed[0:amount // 2 * 2:2], mixed[1:amount // 2 * 2:2]
    slack = jnp.minimum(tallies[donor] - 1, limit - tallies[sink]) // 2
    slack = jnp.where((donor == order[0]) | (sink == order[0]) | (tallies[sink] == 0), 0, jnp.maximum(slack, 0))
    shifted = jax.random.randint(jax.random.fold_in(own, 4), (amount // 2,), 0, 1 << 20) % (slack + 1)
    tallies = tallies.at[donor].add(-shifted).at[sink].add(shifted)
    items = jnp.searchsorted(jnp.cumsum(tallies), jnp.arange(rows * top), side="right").astype(jnp.int32)
    grid = items.reshape(top, rows).T
    grid = grid[jax.random.permutation(jax.random.fold_in(own, 1), rows)]
    rotation = jax.random.randint(jax.random.fold_in(own, 2), (rows, 1), 0, top)
    return jnp.take_along_axis(grid, (jnp.arange(top)[None, :] + rotation) % top, axis=1)


def shares(count, total, limit, slope, full):
    loads = [(1 << 20) // math.isqrt(grade ** slope) + 1 for grade in range(1, count + 1)]
    largest = limit if full else min(limit, max(-(-total // count), total * loads[0] // sum(loads)))
    least = 1 if total - largest >= count - 1 else 0
    counts, spare = [largest] + [least] * (count - 1), total - largest - least * (count - 1)
    while spare > 0:
        candidates = [i for i in range(1, count) if counts[i] < largest] or [i for i in range(1, count) if counts[i] < limit]
        pool, budget = sum([loads[i] for i in candidates]), spare
        for i in candidates:
            extra = min(limit - counts[i], max(1, budget * loads[i] // pool), spare)
            counts[i] = counts[i] + extra
            spare = spare - extra
    return np.array(counts)


def centred(stream_key, extent, scale, most, cuts=(), kind=jnp.bfloat16):
    drawn = scale * jax.random.normal(stream_key, extent, jnp.float32)
    if cuts:
        drawn = drawn * steps_of(stream_key, extent, cuts, -0.22, 0.18)
    return jnp.clip(drawn, -most, most).astype(kind)


def setup_inputs(seed: int = 0) -> dict:
    streams_of = jax.random.split(jax.random.key(seed), 9)
    frames = centred(streams_of[0], (REC, FRAMES, D), 1.0, 6.0, ((0, 4), (1, 32)))
    cotangent = centred(streams_of[1], (REC, FRAMES, D), 1.0, 6.0, ((0, 4), (1, 32)))
    routes_keys = jax.random.split(jax.random.fold_in(streams_of[2], 1), REC * FRAMES // FR_DEV)
    routes_turns = jax.random.permutation(jax.random.fold_in(streams_of[2], 3), REC * FRAMES // FR_DEV)
    routes = jax.vmap(lambda own, number: assign_block(jax.random.fold_in(streams_of[2], 2), own, number, FR_DEV, EXPERTS, 1, CAP, 2))(routes_keys, routes_turns).reshape((REC, FRAMES, 1))
    lengths = draw_lengths(jax.random.fold_in(streams_of[8], 71), 0)
    conv_weight = centred(streams_of[4], (KERNEL, D), 0.15, 0.875, (), jnp.float32)
    norm_gain = jnp.clip(1.0 + 0.15 * jax.random.normal(streams_of[5], (D,), jnp.float32), 0.25, 1.75)
    expert_in = centred(streams_of[6], (EXPERTS, D, H), D ** -0.5, 0.21875, ((0, 128),))
    expert_out = centred(streams_of[7], (EXPERTS, H, D), H ** -0.5, 0.109375, ((0, 128),))
    return {"frames": frames, "cotangent": cotangent, "routes": routes, "lengths": lengths, "conv_weight": conv_weight, "norm_gain": norm_gain, "expert_in": expert_in, "expert_out": expert_out}


def depthwise(padded, weight, count):
    total = jnp.zeros(padded.shape[:-2] + (count, padded.shape[-1]), jnp.float32)
    for offset in range(weight.shape[0]):
        window = lax.slice_in_dim(padded, offset, offset + count, axis=padded.ndim - 2)
        total = total + weight[offset] * window.astype(jnp.float32)
    return total

def expert_pass(operands):
    rows_in, rows_grad, weight_in, weight_out = operands
    pre_act = jnp.dot(rows_in, weight_in, preferred_element_type=jnp.float32)
    hidden_act = jax.nn.silu(pre_act).astype(jnp.bfloat16)
    result = jnp.dot(hidden_act, weight_out, preferred_element_type=jnp.float32).astype(jnp.bfloat16)
    d_act = jnp.dot(rows_grad, weight_out.T, preferred_element_type=jnp.float32)
    sigmoid = jax.nn.sigmoid(pre_act)
    d_pre = (d_act * sigmoid * (1.0 + pre_act * (1.0 - sigmoid))).astype(jnp.bfloat16)
    grad_out = jnp.dot(hidden_act.T, rows_grad, preferred_element_type=jnp.float32).astype(jnp.bfloat16)
    grad_in = jnp.dot(rows_in.T, d_pre, preferred_element_type=jnp.float32).astype(jnp.bfloat16)
    d_rows = jnp.dot(d_pre, weight_in.T, preferred_element_type=jnp.float32).astype(jnp.bfloat16)
    return (result, d_rows, grad_in, grad_out)

def reference(frames, cotangent, routes, lengths, conv_weight, norm_gain, expert_in, expert_out):
    reach = (KERNEL - 1) // 2
    frame_index = jnp.arange(FRAMES, dtype=jnp.int32)
    in_range = (frame_index[None, :] < lengths[:, None]).astype(jnp.float32)[:, :, None]
    masked = frames * in_range.astype(jnp.bfloat16)
    padded = jnp.pad(masked, ((0, 0), (reach, reach), (0, 0)))
    conv_out = masked.astype(jnp.float32) + depthwise(padded, conv_weight, FRAMES)
    inv_rms = lax.rsqrt(lax.optimization_barrier(jnp.mean(conv_out * conv_out, axis=-1, keepdims=True)) + 1e-05)
    normed = conv_out * inv_rms
    hidden_in = (normed * norm_gain).astype(jnp.bfloat16)
    grad_rows = cotangent * in_range.astype(jnp.bfloat16)
    sources = REC * (FRAMES // FR_DEV)
    expert_ids = routes.reshape(sources, FR_DEV)
    onehot = (expert_ids[:, :, None] == jnp.arange(EXPERTS, dtype=jnp.int32)[None, None, :]).astype(jnp.int32)
    slot_index = lax.optimization_barrier(jnp.sum((jnp.cumsum(onehot, axis=1) - 1) * onehot, axis=2))
    source_ids = jnp.arange(sources, dtype=jnp.int32)[:, None]
    target = ((expert_ids * sources + source_ids) * CAP + slot_index).reshape(-1).astype(jnp.int32)
    buffer_in = jnp.zeros((EXPERTS * sources * CAP, D), jnp.bfloat16).at[target].set(hidden_in.reshape(-1, D))
    buffer_grad = jnp.zeros((EXPERTS * sources * CAP, D), jnp.bfloat16).at[target].set(grad_rows.reshape(-1, D))
    buffer_in = buffer_in.reshape(EXPERTS, sources * CAP, D)
    buffer_grad = buffer_grad.reshape(EXPERTS, sources * CAP, D)
    results, d_rows, grad_in, grad_out = lax.map(expert_pass, (buffer_in, buffer_grad, expert_in, expert_out))
    back_rows = results.reshape(-1, D)[target].reshape(REC, FRAMES, D)
    d_hidden = d_rows.reshape(-1, D)[target].reshape(REC, FRAMES, D)
    output = (conv_out + in_range * back_rows.astype(jnp.float32)).astype(jnp.bfloat16)
    scale = 1.0 / math.sqrt(REC * FRAMES)
    d_hidden_f = d_hidden.astype(jnp.float32)
    d_normed = d_hidden_f * norm_gain
    d_conv = cotangent.astype(jnp.float32) + inv_rms * (d_normed - normed * lax.optimization_barrier(jnp.mean(d_normed * normed, axis=-1, keepdims=True)))
    grad_gain = scale * lax.optimization_barrier(jnp.sum(d_hidden_f * normed, axis=(0, 1)))
    taps = []
    for offset in range(KERNEL):
        window = lax.slice_in_dim(padded, offset, offset + FRAMES, axis=1).astype(jnp.float32)
        taps.append(lax.optimization_barrier(jnp.sum(d_conv * window, axis=(0, 1))))
    grad_conv = scale * jnp.stack(taps)
    d_padded = jnp.pad(d_conv, ((0, 0), (reach, reach), (0, 0)))
    d_masked = d_conv + depthwise(d_padded, conv_weight[::-1], FRAMES)
    grad_frames = (in_range * d_masked).astype(jnp.bfloat16)
    return (output, grad_frames, grad_conv, grad_gain, grad_in, grad_out)
```

```python
import math

import jax
import jax.numpy as jnp
from jax import lax
from jax.experimental import pallas as pl
from jax.experimental.pallas import tpu as pltpu
from jax.sharding import PartitionSpec as P

LANES = 128
EDGE = 16
ROWS = 64
SLOTS = 4
PAIR = 2 * SLOTS
VMEM = pl.BlockSpec(memory_space=pltpu.VMEM)
SMEM = pl.BlockSpec(memory_space=pltpu.SMEM)
BIG = pltpu.CompilerParams(vmem_limit_bytes=48 * 1024 * 1024)


def f32(x):
    return x.astype(jnp.float32)


def bf16(x):
    return x.astype(jnp.bfloat16)


def dot(a, b, dims=((1,), (0,))):
    return lax.dot_general(a, b, (dims, ((), ())), preferred_element_type=jnp.float32)


def iota(shape, axis):
    return lax.broadcasted_iota(jnp.int32, shape, axis)


def cost(flops, nbytes):
    return pl.CostEstimate(flops=flops, bytes_accessed=nbytes, transcendentals=0)


def pre_kernel(
    nv_ref, col_ref, row_ref, x_ref, left_ref, right_ref, cot_ref, w_ref, gain_ref,
    send_ref, conv_ref, inv_ref, pad_ref,
    stack, taps, squares,
):
    count, width = x_ref.shape
    chunks = width // LANES
    reach = (w_ref.shape[0] - 1) // 2
    valid = nv_ref[0]
    edge = iota((EDGE, LANES), 0)
    inside = iota((count, LANES), 0) < valid
    for c in range(chunks):
        lanes = slice(c * LANES, (c + 1) * LANES)
        pad_ref[c, 0:EDGE, :] = jnp.where(edge - EDGE < valid, f32(left_ref[:, lanes]), 0.0)
        pad_ref[c, EDGE : EDGE + count, :] = jnp.where(inside, f32(x_ref[:, lanes]), 0.0)
        pad_ref[c, EDGE + count :, :] = jnp.where(edge + count < valid, f32(right_ref[:, lanes]), 0.0)
        taps[c, 0 : w_ref.shape[0], :] = w_ref[:, lanes]
        stack[count:, lanes] = bf16(jnp.where(inside, f32(cot_ref[:, lanes]), 0.0))
    squares[...] = jnp.zeros_like(squares)

    @pl.loop(0, chunks)
    def _(c):
        for start in range(0, count, ROWS):
            total = jnp.zeros((ROWS, LANES), jnp.float32)
            for k in range(w_ref.shape[0]):
                at = start + k + EDGE - reach
                total = total + taps[c, k : k + 1, :] * pad_ref[c, at : at + ROWS, :]
            total = pad_ref[c, EDGE + start : EDGE + start + ROWS, :] + total
            conv_ref[c, start : start + ROWS, :] = total
            squares[start : start + ROWS, :] += total * total

    inv = lax.rsqrt(jnp.sum(squares[...], axis=-1, keepdims=True) * (1.0 / width) + 1e-05)
    inv = jnp.broadcast_to(inv, (count, LANES))
    inv_ref[...] = inv
    for c in range(chunks):
        lanes = slice(c * LANES, (c + 1) * LANES)
        stack[0:count, lanes] = bf16(conv_ref[c] * inv * gain_ref[:, lanes])

    earlier = (col_ref[...] == row_ref[...]) & (iota((count, count), 0) < iota((count, count), 1))
    slot = jnp.sum(jnp.where(earlier, 1.0, 0.0), axis=0, keepdims=True).astype(jnp.int32)
    key = row_ref[...] * PAIR + slot
    key = jnp.concatenate([key, key + SLOTS], axis=1)
    block = 256
    for start in range(0, send_ref.shape[0], block):
        pick = bf16(jnp.where(iota((block, 2 * count), 0) + start == key, 1.0, 0.0))
        send_ref[start : start + block, :] = bf16(dot(pick, stack[...]))


def expert_kernel(recv_ref, win_ref, wout_ref, back_ref, x_ref, g_ref, act_ref, dpre_ref):
    rows, width = x_ref.shape
    hidden = win_ref.shape[1]
    half, whole = 128, 256
    i, r = iota((half, whole), 0), iota((half, whole), 1)
    place = (i // SLOTS) * PAIR + i % SLOTS
    pick_x = bf16(jnp.where(r == place, 1.0, 0.0))
    pick_g = bf16(jnp.where(r == place + SLOTS, 1.0, 0.0))
    for n in range(rows // half):
        part = recv_ref[n * whole : (n + 1) * whole, :]
        x_ref[n * half : (n + 1) * half, :] = bf16(dot(pick_x, part))
        g_ref[n * half : (n + 1) * half, :] = bf16(dot(pick_g, part))
    result = jnp.zeros((rows, width), jnp.float32)
    d_rows = jnp.zeros((rows, width), jnp.float32)
    tile = 512
    for start in range(0, hidden, tile):
        cols = slice(start, start + tile)
        pre = dot(x_ref[...], win_ref[:, cols])
        d_act = dot(g_ref[...], wout_ref[cols, :], ((1,), (1,)))
        gate = jax.nn.sigmoid(pre)
        act = bf16(pre * gate)
        d_pre = bf16(d_act * gate * (1.0 + pre * (1.0 - gate)))
        act_ref[:, cols] = act
        dpre_ref[:, cols] = d_pre
        result = result + dot(act, wout_ref[cols, :])
        d_rows = d_rows + dot(d_pre, win_ref[:, cols], ((1,), (1,)))
    result, d_rows = bf16(result), bf16(d_rows)
    q, j = iota((whole, half), 0), iota((whole, half), 1)
    home = (j // SLOTS) * PAIR + j % SLOTS
    put_x = bf16(jnp.where(q == home, 1.0, 0.0))
    put_g = bf16(jnp.where(q == home + SLOTS, 1.0, 0.0))
    for n in range(rows // half):
        part = slice(n * half, (n + 1) * half)
        back_ref[n * whole : (n + 1) * whole, :] = bf16(
            dot(put_x, result[part, :]) + dot(put_g, d_rows[part, :])
        )


def grads_kernel(x_ref, g_ref, act_ref, dpre_ref, gin_ref, gout_ref):
    gin_ref[0] = bf16(dot(x_ref[...], dpre_ref[...], ((0,), (0,))))
    gout_ref[0] = bf16(dot(act_ref[...], g_ref[...], ((0,), (0,))))


def post_kernel(
    nv_ref, col_ref, row_ref, recv_ref, conv_ref, inv_ref, pad_ref, cot_ref, gain_ref,
    out_ref, dconv_ref, head_ref, tail_ref, sums_ref,
    back, dhid, means,
):
    count, width = cot_ref.shape
    chunks = width // LANES
    kernel = sums_ref.shape[0] - 1
    reach = (kernel - 1) // 2
    earlier = (col_ref[...] == row_ref[...]) & (iota((count, count), 1) < iota((count, count), 0))
    slot = jnp.sum(jnp.where(earlier, 1.0, 0.0), axis=1, keepdims=True).astype(jnp.int32)
    key = col_ref[...] * PAIR + slot
    seats = iota((count, recv_ref.shape[0]), 1)
    dhid[...] = dot(bf16(jnp.where(seats == key + SLOTS, 1.0, 0.0)), recv_ref[...])
    back[...] = dot(bf16(jnp.where(seats == key, 1.0, 0.0)), recv_ref[...])
    inside = iota((count, LANES), 0) < nv_ref[0]
    inv = inv_ref[...]
    means[...] = jnp.zeros_like(means)
    for c in range(chunks):
        lanes = slice(c * LANES, (c + 1) * LANES)
        normed = conv_ref[c] * inv
        d_hidden = dhid[:, lanes]
        means[...] += d_hidden * gain_ref[:, lanes] * normed
        sums_ref[kernel : kernel + 1, lanes] = jnp.sum(d_hidden * normed, axis=0, keepdims=True)
        out_ref[:, lanes] = bf16(conv_ref[c] + jnp.where(inside, back[:, lanes], 0.0))
    mean = jnp.sum(means[...], axis=-1, keepdims=True) * (1.0 / width)
    mean = jnp.broadcast_to(mean, (count, LANES))
    for c in range(chunks):
        lanes = slice(c * LANES, (c + 1) * LANES)
        d_conv = f32(cot_ref[:, lanes]) + inv * (
            dhid[:, lanes] * gain_ref[:, lanes] - conv_ref[c] * inv * mean
        )
        dconv_ref[c] = d_conv
        head_ref[c] = d_conv[0:EDGE, :]
        tail_ref[c] = d_conv[count - EDGE :, :]
    for c in range(chunks):
        lanes = slice(c * LANES, (c + 1) * LANES)
        totals = [jnp.zeros((8, LANES), jnp.float32) for _ in range(kernel)]
        for start in range(0, count, ROWS):
            part = dconv_ref[c, start : start + ROWS, :]
            for k in range(kernel):
                at = start + k + EDGE - reach
                product = part * pad_ref[c, at : at + ROWS, :]
                totals[k] = totals[k] + jnp.sum(product.reshape(ROWS // 8, 8, LANES), axis=0)
        for k in range(kernel):
            sums_ref[k : k + 1, lanes] = jnp.sum(totals[k], axis=0, keepdims=True)


def back_kernel(nv_ref, dconv_ref, left_ref, right_ref, w_ref, grad_ref, pad, taps):
    chunks, count, _ = dconv_ref.shape
    kernel = w_ref.shape[0]
    reach = (kernel - 1) // 2
    for c in range(chunks):
        pad[c, 0:EDGE, :] = left_ref[c]
        pad[c, EDGE : EDGE + count, :] = dconv_ref[c]
        pad[c, EDGE + count :, :] = right_ref[c]
    valid = nv_ref[0]
    for c in range(chunks):
        lanes = slice(c * LANES, (c + 1) * LANES)
        for start in range(0, count, ROWS):
            total = jnp.zeros((ROWS, LANES), jnp.float32)
            for k in range(kernel):
                at = start + EDGE + reach - k
                total = total + w_ref[k : k + 1, lanes] * pad[c, at : at + ROWS, :]
            total = pad[c, EDGE + start : EDGE + start + ROWS, :] + total
            keep = iota((ROWS, LANES), 0) + start < valid
            grad_ref[start : start + ROWS, lanes] = bf16(jnp.where(keep, total, 0.0))


def ring_sum(part, axis, pairs_of):
    one, two, three = (lax.ppermute(part, axis, pairs_of(flip)) for flip in (1, 2, 3))
    return (part + one) + (two + three)


def total_over_all(sums):
    rows = sums.shape[0] // 2
    n_tm = lax.axis_size("tm")
    core = lax.axis_index("tm") % 2
    swap = [(i, i ^ 1) for i in range(n_tm)]
    mine = lax.dynamic_slice_in_dim(sums, core * rows, rows, 0)
    other = lax.dynamic_slice_in_dim(sums, (1 - core) * rows, rows, 0)
    part = mine + lax.ppermute(other, "tm", swap)
    part = ring_sum(part, "tm", lambda f: [(i, i ^ (2 * f)) for i in range(n_tm)])
    part = ring_sum(part, "rec", lambda f: [(i, i ^ f) for i in range(4)])
    part = ring_sum(part, "tm", lambda f: [(i, i ^ (8 * f)) for i in range(n_tm)])
    part = part * (1.0 / math.sqrt(lax.axis_size("rec") * n_tm * 384))
    fellow = lax.ppermute(part, "tm", swap)
    low = jnp.where(core == 0, part, fellow)
    high = jnp.where(core == 0, fellow, part)
    return jnp.concatenate([low, high], axis=0)


def shifted(tail, head):
    n = lax.axis_size("tm")
    left = lax.ppermute(tail, "tm", [(i, i + 1) for i in range(n - 1)])
    right = lax.ppermute(head, "tm", [(i + 1, i) for i in range(n - 1)])
    return left, right


def local(frames, cotangent, routes, lengths, conv_weight, norm_gain, expert_in, expert_out):
    count, width = frames.shape[1:]
    kernel = conv_weight.shape[0]
    chunks = width // LANES
    devices = lax.axis_size("rec") * lax.axis_size("tm")
    hidden = expert_in.shape[2]
    rows = devices * SLOTS
    x, cot = frames[0], cotangent[0]
    win, wout = expert_in[0], expert_out[0]
    gain = norm_gain[None, :]
    valid = lengths - lax.axis_index("tm") * count
    col, row = routes[0], routes[0].reshape(1, count)
    left, right = shifted(x[count - EDGE :], x[:EDGE])
    shape = jax.ShapeDtypeStruct
    wide = shape((chunks, count, LANES), jnp.float32)
    send, conv, inv, pad = pl.pallas_call(
        pre_kernel,
        out_shape=[
            shape((2 * rows, width), jnp.bfloat16),
            wide,
            shape((count, LANES), jnp.float32),
            shape((chunks, count + 2 * EDGE, LANES), jnp.float32),
        ],
        in_specs=[SMEM] + [VMEM] * 8,
        out_specs=[VMEM] * 4,
        scratch_shapes=[
            pltpu.VMEM((2 * count, width), jnp.bfloat16),
            pltpu.VMEM((chunks, 32, LANES), jnp.float32),
            pltpu.VMEM((count, LANES), jnp.float32),
        ],
        compiler_params=BIG,
        cost_estimate=cost(10**9, 10**7),
        name="pre",
    )(valid, col, row, x, left, right, cot, conv_weight, gain)
    recv = lax.all_to_all(send, ("rec", "tm"), split_axis=0, concat_axis=0, tiled=True)
    back, rows_x, rows_g, act, d_pre = pl.pallas_call(
        expert_kernel,
        out_shape=[
            shape((2 * rows, width), jnp.bfloat16),
            shape((rows, width), jnp.bfloat16),
            shape((rows, width), jnp.bfloat16),
            shape((rows, hidden), jnp.bfloat16),
            shape((rows, hidden), jnp.bfloat16),
        ],
        in_specs=[VMEM] * 3,
        out_specs=[VMEM] * 5,
        compiler_params=BIG,
        cost_estimate=cost(8 * rows * width * hidden, 2 * 10**7),
        name="experts",
    )(recv, win, wout)
    home = lax.all_to_all(back, ("rec", "tm"), split_axis=0, concat_axis=0, tiled=True)
    tile = 512
    grad_in, grad_out = pl.pallas_call(
        grads_kernel,
        grid=(hidden // tile,),
        out_shape=[
            shape((1, width, hidden), jnp.bfloat16),
            shape((1, hidden, width), jnp.bfloat16),
        ],
        in_specs=[
            pl.BlockSpec((rows, width), lambda i: (0, 0)),
            pl.BlockSpec((rows, width), lambda i: (0, 0)),
            pl.BlockSpec((rows, tile), lambda i: (0, i)),
            pl.BlockSpec((rows, tile), lambda i: (0, i)),
        ],
        out_specs=[
            pl.BlockSpec((1, width, tile), lambda i: (0, 0, i)),
            pl.BlockSpec((1, tile, width), lambda i: (0, i, 0)),
        ],
        compiler_params=BIG,
        cost_estimate=cost(4 * rows * width * hidden, 2 * 10**7),
        name="weight_grads",
    )(rows_x, rows_g, act, d_pre)
    output, d_conv, head, tail, sums = pl.pallas_call(
        post_kernel,
        out_shape=[
            shape((count, width), jnp.bfloat16),
            wide,
            shape((chunks, EDGE, LANES), jnp.float32),
            shape((chunks, EDGE, LANES), jnp.float32),
            shape((kernel + 1, width), jnp.float32),
        ],
        in_specs=[SMEM] + [VMEM] * 8,
        out_specs=[VMEM] * 5,
        scratch_shapes=[
            pltpu.VMEM((count, width), jnp.float32),
            pltpu.VMEM((count, width), jnp.float32),
            pltpu.VMEM((count, LANES), jnp.float32),
        ],
        compiler_params=BIG,
        cost_estimate=cost(10**9, 10**7),
        name="post",
    )(valid, col, row, home, conv, inv, pad, cot, gain)
    left, right = shifted(tail, head)
    grad_frames = pl.pallas_call(
        back_kernel,
        out_shape=shape((count, width), jnp.bfloat16),
        in_specs=[SMEM] + [VMEM] * 4,
        out_specs=VMEM,
        scratch_shapes=[
            pltpu.VMEM((chunks, count + 2 * EDGE, LANES), jnp.float32),
            pltpu.VMEM((chunks, 32, LANES), jnp.float32),
        ],
        compiler_params=BIG,
        cost_estimate=cost(10**9, 10**7),
        name="conv_back",
    )(valid, d_conv, left, right, conv_weight)
    total = total_over_all(sums)
    return (
        output[None],
        grad_frames[None],
        total[:kernel],
        total[kernel],
        grad_in,
        grad_out,
    )


def solution(mesh):
    placed = (
        P("rec", "tm", None),
        P("rec", "tm", None),
        P("rec", "tm", None),
        P("rec"),
        P(),
        P(),
        P(("rec", "tm"), None, None),
        P(("rec", "tm"), None, None),
    )
    return jax.shard_map(
        local,
        mesh=mesh,
        in_specs=placed,
        out_specs=(
            P("rec", "tm", None),
            P("rec", "tm", None),
            P(),
            P(),
            P(("rec", "tm"), None, None),
            P(("rec", "tm"), None, None),
        ),
        check_vma=False,
    )
```

```python
import functools
import math

import jax
import jax.numpy as jnp
from jax import lax
from jax.experimental import pallas as pl
from jax.experimental.pallas import tpu as pltpu
from jax.sharding import PartitionSpec as P

LANES = 128
EDGE = 16
ROWS = 64
SLOTS = 4
PAIR = 2 * SLOTS
VMEM = pl.BlockSpec(memory_space=pltpu.VMEM)
SMEM = pl.BlockSpec(memory_space=pltpu.SMEM)
ANY = pl.BlockSpec(memory_space=pl.ANY)
HBM = pl.BlockSpec(memory_space=pltpu.HBM)


def f32(x):
    return x.astype(jnp.float32)


def bf16(x):
    return x.astype(jnp.bfloat16)


def dot(a, b, dims=((1,), (0,))):
    return lax.dot_general(a, b, (dims, ((), ())), preferred_element_type=jnp.float32)


def iota(shape, axis):
    return lax.broadcasted_iota(jnp.int32, shape, axis)


def limit(mebibytes):
    return pltpu.CompilerParams(vmem_limit_bytes=mebibytes * 1024 * 1024)


def hbm(x):
    return pltpu.with_memory_space_constraint(x, pltpu.HBM)


def cost(flops, nbytes):
    return pl.CostEstimate(flops=flops, bytes_accessed=nbytes, transcendentals=0)


def pre_kernel(
    nv_ref, row_hbm, x_hbm, cot_hbm, w_hbm, gain_hbm,
    conv_ref, pad_ref, squares_ref, pick_ref, send_ref, taps_ref,
    row_ref, x_ref, cot_ref, w_ref, gain_ref, grads, sems,
):
    count, width = x_ref.shape
    chunks = width // LANES
    kernel = w_ref.shape[0]
    reach = (kernel - 1) // 2
    copies = [
        pltpu.make_async_copy(src, dst, sems.at[i])
        for i, (src, dst) in enumerate(
            (
                (x_hbm, x_ref), (w_hbm, w_ref), (gain_hbm, gain_ref),
                (row_hbm, row_ref), (cot_hbm, cot_ref),
            )
        )
    ]
    for copy in copies:
        copy.start()
    valid = nv_ref[0]
    inside = iota((count, LANES), 0) < valid
    squares_ref[...] = jnp.zeros_like(squares_ref)
    for copy in copies[:3]:
        copy.wait()
    for c in range(chunks):
        lanes = slice(c * LANES, (c + 1) * LANES)
        pad_ref[c, 0:EDGE, :] = jnp.zeros((EDGE, LANES), jnp.float32)
        pad_ref[c, EDGE : EDGE + count, :] = jnp.where(inside, f32(x_ref[:, lanes]), 0.0)
        pad_ref[c, EDGE + count :, :] = jnp.zeros((EDGE, LANES), jnp.float32)
        taps_ref[c, 0:kernel, :] = w_ref[:, lanes]
        taps_ref[c, kernel : kernel + 1, :] = gain_ref[lanes][None, :]

    @pl.loop(0, chunks)
    def _(c):
        for start in range(0, count, ROWS):
            total = jnp.zeros((ROWS, LANES), jnp.float32)
            for k in range(kernel):
                at = start + k + EDGE - reach
                total = total + taps_ref[c, k : k + 1, :] * pad_ref[c, at : at + ROWS, :]
            total = pad_ref[c, EDGE + start : EDGE + start + ROWS, :] + total
            conv_ref[c, start : start + ROWS, :] = total
            if 0 < start < count - ROWS:
                squares_ref[start : start + ROWS, :] += total * total
            else:
                low = EDGE if start == 0 else 0
                high = ROWS if start == 0 else ROWS - EDGE
                inner = total[low:high, :]
                squares_ref[start + low : start + high, :] += inner * inner

    for copy in copies[3:]:
        copy.wait()
    row = row_ref[...]
    experts = send_ref.shape[0] // PAIR
    named = jnp.where(iota((experts, count), 0) == row, 1.0, 0.0)
    before = bf16(jnp.where(iota((count, count), 0) < iota((count, count), 1), 1.0, 0.0))
    slot = jnp.sum(named * dot(bf16(named), before), axis=0, keepdims=True)
    key = row * PAIR + slot.astype(jnp.int32)
    for c in range(chunks):
        lanes = slice(c * LANES, (c + 1) * LANES)
        grads[:, lanes] = bf16(jnp.where(inside, f32(cot_ref[:, lanes]), 0.0))
    block = 256
    for start in range(0, send_ref.shape[0], block):
        seat = iota((block, count), 0) + start
        pick_ref[start : start + block, :] = bf16(jnp.where(seat == key, 1.0, 0.0))
        pick = bf16(jnp.where(seat == key + SLOTS, 1.0, 0.0))
        send_ref[start : start + block, :] = bf16(dot(pick, grads[...]))


def send_kernel(
    nv_ref, left_ref, right_ref, conv_in, pad_in, squares_ref, pick_ref, grads_ref, taps_ref,
    conv_ref, pad_ref, send_ref, inv_ref,
    rows, squares,
):
    chunks, count, _ = conv_in.shape
    width = chunks * LANES
    kernel = taps_ref.shape[1] - 1
    reach = (kernel - 1) // 2
    valid = nv_ref[0]
    edge = iota((EDGE, LANES), 0)
    squares[...] = squares_ref[...]
    for c in range(chunks):
        lanes = slice(c * LANES, (c + 1) * LANES)
        pad_ref[c, 0:EDGE, :] = jnp.where(edge - EDGE < valid, f32(left_ref[:, lanes]), 0.0)
        pad_ref[c, EDGE : EDGE + count, :] = pad_in[c, EDGE : EDGE + count, :]
        pad_ref[c, EDGE + count :, :] = jnp.where(edge + count < valid, f32(right_ref[:, lanes]), 0.0)
        conv_ref[c, EDGE : count - EDGE, :] = conv_in[c, EDGE : count - EDGE, :]
        for start in (0, count - EDGE):
            total = jnp.zeros((EDGE, LANES), jnp.float32)
            for k in range(kernel):
                at = start + k + EDGE - reach
                total = total + taps_ref[c, k : k + 1, :] * pad_ref[c, at : at + EDGE, :]
            total = pad_ref[c, EDGE + start : EDGE + start + EDGE, :] + total
            conv_ref[c, start : start + EDGE, :] = total
            squares[start : start + EDGE, :] += total * total
    inv = lax.rsqrt(jnp.sum(squares[...], axis=-1, keepdims=True) * (1.0 / width) + 1e-05)
    inv = jnp.broadcast_to(inv, (count, LANES))
    inv_ref[...] = inv
    for c in range(chunks):
        lanes = slice(c * LANES, (c + 1) * LANES)
        rows[:, lanes] = bf16(conv_ref[c] * inv * taps_ref[c, kernel : kernel + 1, :])
    block = 256
    for start in range(0, send_ref.shape[0], block):
        part = slice(start, start + block)
        send_ref[part, :] = bf16(dot(pick_ref[part, :], rows[...]) + f32(grads_ref[part, :]))


def picks():
    half, whole = 128, 256
    i, r = iota((half, whole), 0), iota((half, whole), 1)
    place = (i // SLOTS) * PAIR + i % SLOTS
    return bf16(jnp.where(r == place, 1.0, 0.0)), bf16(jnp.where(r == place + SLOTS, 1.0, 0.0))


def unpack(recv_ref, x_ref, g_ref, copies=None):
    pick_x, pick_g = picks()
    half, whole = pick_x.shape
    for n in range(x_ref.shape[0] // half):
        if copies:
            copies[n].wait()
        part = recv_ref[n * whole : (n + 1) * whole, :]
        x_ref[n * half : (n + 1) * half, :] = bf16(dot(pick_x, part))
        g_ref[n * half : (n + 1) * half, :] = bf16(dot(pick_g, part))


TILE = 512


def expert_kernel(
    recv_hbm, win_hbm, wout_hbm,
    back_hbm, act_hbm, dpre_hbm,
    recv_ref, win_ref, wout_ref, x_ref, g_ref, act_ref, dpre_ref, result, d_rows,
    row_sems, in_sems, out_sems,
):
    rows = x_ref.shape[0]
    hidden = win_ref.shape[1]
    tiles = hidden // TILE
    half, whole = 128, 256
    groups = rows // half
    arrivals, returns, loads, stores = [], [], [], []
    for n in range(groups):
        part = pl.ds(n * whole, whole)
        arrivals.append(pltpu.make_async_copy(recv_hbm.at[part, :], recv_ref.at[part, :], row_sems.at[0, n]))
        returns.append(pltpu.make_async_copy(recv_ref.at[part, :], back_hbm.at[part, :], row_sems.at[1, n]))
        arrivals[n].start()
    for n in range(tiles):
        cols = pl.ds(n * TILE, TILE)
        loads.append((
            pltpu.make_async_copy(win_hbm.at[:, cols], win_ref.at[:, cols], in_sems.at[0, n]),
            pltpu.make_async_copy(wout_hbm.at[cols, :], wout_ref.at[cols, :], in_sems.at[1, n]),
        ))
        stores.append((
            pltpu.make_async_copy(act_ref.at[:, cols], act_hbm.at[:, cols], out_sems.at[0, n]),
            pltpu.make_async_copy(dpre_ref.at[:, cols], dpre_hbm.at[:, cols], out_sems.at[1, n]),
        ))
        for copy in loads[n]:
            copy.start()
    unpack(recv_ref, x_ref, g_ref, arrivals)

    def front(n):
        cols = slice(n * TILE, (n + 1) * TILE)
        for copy in loads[n]:
            copy.wait()
        return (
            dot(x_ref[...], win_ref[:, cols]),
            dot(g_ref[...], wout_ref[cols, :], ((1,), (1,))),
        )

    ready = front(0)
    for n in range(tiles):
        cols = slice(n * TILE, (n + 1) * TILE)
        pre, d_act = ready
        if n + 1 < tiles:
            ready = front(n + 1)
        gate = 0.5 * jnp.tanh(0.5 * pre) + 0.5
        value = pre * gate
        act = bf16(value)
        d_pre = bf16(d_act * (gate + value * (1.0 - gate)))
        act_ref[:, cols] = act
        dpre_ref[:, cols] = d_pre
        for copy in stores[n]:
            copy.start()
        forward = dot(act, wout_ref[cols, :])
        backward = dot(d_pre, win_ref[:, cols], ((1,), (1,)))
        if n:
            forward, backward = forward + result[...], backward + d_rows[...]
        result[...] = forward
        d_rows[...] = backward
    q, j = iota((whole, half), 0), iota((whole, half), 1)
    home = (j // SLOTS) * PAIR + j % SLOTS
    put_x = bf16(jnp.where(q == home, 1.0, 0.0))
    put_g = bf16(jnp.where(q == home + SLOTS, 1.0, 0.0))
    for n in range(groups):
        part = slice(n * half, (n + 1) * half)
        recv_ref[n * whole : (n + 1) * whole, :] = bf16(
            dot(put_x, bf16(result[part, :])) + dot(put_g, bf16(d_rows[part, :]))
        )
        returns[n].start()
    for pair in stores:
        for copy in pair:
            copy.wait()
    for copy in returns:
        copy.wait()


def grads_kernel(recv_ref, act_ref, dpre_ref, gin_ref, gout_ref, done_ref, x_ref, g_ref):
    @pl.when(pl.program_id(0) == 0)
    def _():
        unpack(recv_ref, x_ref, g_ref)

    gin_ref[0] = bf16(dot(x_ref[...], dpre_ref[...], ((0,), (0,))))
    gout_ref[0] = bf16(dot(act_ref[...], g_ref[...], ((0,), (0,))))
    done_ref[...] = jnp.zeros_like(done_ref)


def post_kernel(
    nv_ref, row_hbm, recv_hbm, cot_hbm, inv_hbm, conv_hbm, taps_hbm, pad_hbm, done_ref,
    out_ref, dconv_ref, head_ref, tail_ref, mine_ref, other_ref,
    row_ref, recv_ref, cot_ref, inv_ref, conv_ref, taps_ref, pad_ref,
    back, dhid, means, sums_ref, sems,
):
    copies = [
        pltpu.make_async_copy(src, dst, sems.at[i])
        for i, (src, dst) in enumerate(
            (
                (row_hbm, row_ref), (recv_hbm, recv_ref), (cot_hbm, cot_ref), (inv_hbm, inv_ref),
                (conv_hbm, conv_ref), (taps_hbm, taps_ref), (pad_hbm, pad_ref),
            )
        )
    ]
    for copy in copies:
        copy.start()
    count, width = cot_ref.shape
    chunks = width // LANES
    kernel = sums_ref.shape[0] - 1
    reach = (kernel - 1) // 2
    here, there = iota((count, count), 0), iota((count, count), 1)
    copies[0].wait()
    row = row_ref[...]
    col = jnp.sum(jnp.where(here == there, f32(row), 0.0), axis=1, keepdims=True).astype(jnp.int32)
    earlier = (col == row) & (there < here)
    slot = jnp.sum(jnp.where(earlier, 1.0, 0.0), axis=1, keepdims=True).astype(jnp.int32)
    key = col * PAIR + slot
    seats = iota((count, recv_ref.shape[0]), 1)
    pick_grad = bf16(jnp.where(seats == key + SLOTS, 1.0, 0.0))
    pick_out = bf16(jnp.where(seats == key, 1.0, 0.0))
    copies[1].wait()
    dhid[...] = dot(pick_grad, recv_ref[...])
    back[...] = dot(pick_out, recv_ref[...])
    for copy in copies[2:]:
        copy.wait()
    inside = iota((count, LANES), 0) < nv_ref[0]
    inv = inv_ref[...]
    means[...] = jnp.zeros_like(means)
    for c in range(chunks):
        lanes = slice(c * LANES, (c + 1) * LANES)
        normed = conv_ref[c] * inv
        d_hidden = dhid[:, lanes]
        means[...] += d_hidden * taps_ref[c, kernel : kernel + 1, :] * normed
        sums_ref[kernel : kernel + 1, lanes] = jnp.sum(d_hidden * normed, axis=0, keepdims=True)
        out_ref[:, lanes] = bf16(conv_ref[c] + jnp.where(inside, back[:, lanes], 0.0))
    mean = jnp.sum(means[...], axis=-1, keepdims=True) * (1.0 / width)
    mean = jnp.broadcast_to(mean, (count, LANES))
    for c in range(chunks):
        lanes = slice(c * LANES, (c + 1) * LANES)
        d_conv = f32(cot_ref[:, lanes]) + inv * (
            dhid[:, lanes] * taps_ref[c, kernel : kernel + 1, :] - conv_ref[c] * inv * mean
        )
        dconv_ref[c] = d_conv
        head_ref[c] = d_conv[0:EDGE, :]
        tail_ref[c] = d_conv[count - EDGE :, :]
    for c in range(chunks):
        lanes = slice(c * LANES, (c + 1) * LANES)
        totals = [jnp.zeros((8, LANES), jnp.float32) for _ in range(kernel)]
        for start in range(0, count, ROWS):
            part = dconv_ref[c, start : start + ROWS, :]
            for k in range(kernel):
                at = start + k + EDGE - reach
                product = part * pad_ref[c, at : at + ROWS, :]
                totals[k] = totals[k] + jnp.sum(product.reshape(ROWS // 8, 8, LANES), axis=0)
        for k in range(kernel):
            sums_ref[k : k + 1, lanes] = jnp.sum(totals[k], axis=0, keepdims=True)
    core = nv_ref[1]
    rows = mine_ref.shape[0]
    low, high = sums_ref[0:rows, :], sums_ref[rows:, :]
    mine_ref[...] = jnp.where(core == 0, low, high)
    other_ref[...] = jnp.where(core == 0, high, low)


def back_kernel(first, nv_ref, dconv_ref, left_ref, right_ref, taps_ref, tie_ref, grad_ref, low, high):
    _, count, _ = dconv_ref.shape
    kernel = taps_ref.shape[1] - 1
    reach = (kernel - 1) // 2
    valid = nv_ref[0]
    for i in range(grad_ref.shape[1] // LANES):
        c = first + i
        lanes = slice(i * LANES, (i + 1) * LANES)
        low[i, 0:EDGE, :] = left_ref[c]
        low[i, EDGE:, :] = dconv_ref[c, 0 : ROWS + EDGE, :]
        high[i, 0 : ROWS + EDGE, :] = dconv_ref[c, count - ROWS - EDGE :, :]
        high[i, ROWS + EDGE :, :] = right_ref[c]
        for start in range(0, count, ROWS):
            if start == 0:
                window, shift, at = low, EDGE, i
            elif start == count - ROWS:
                window, shift, at = high, EDGE - start, i
            else:
                window, shift, at = dconv_ref, 0, c
            total = jnp.zeros((ROWS, LANES), jnp.float32)
            for k in range(kernel):
                begin = start + shift + reach - k
                total = total + taps_ref[c, k : k + 1, :] * window[at, begin : begin + ROWS, :]
            total = window[at, start + shift : start + shift + ROWS, :] + total
            keep = iota((ROWS, LANES), 0) + start < valid
            grad_ref[start : start + ROWS, lanes] = bf16(jnp.where(keep, total, 0.0))


def add_kernel(tie_ref, own_ref, one_ref, two_ref, three_ref, out_ref):
    out_ref[...] = (own_ref[...] + one_ref[...]) + (two_ref[...] + three_ref[...])


def finish_kernel(scale, nv_ref, part_ref, fellow_ref, *refs):
    pieces, (taps_ref, gain_ref, grad_ref) = refs[:-3], refs[-3:]
    core = nv_ref[1]
    rows = part_ref.shape[0]
    part, fellow = part_ref[...] * scale, fellow_ref[...] * scale
    low = jnp.where(core == 0, part, fellow)
    high = jnp.where(core == 0, fellow, part)
    taps_ref[0:rows, :] = low
    taps_ref[rows:, :] = high[0 : rows - 1, :]
    gain_ref[...] = high[rows - 1, :]
    width = pieces[0].shape[1]
    for n, piece in enumerate(pieces):
        grad_ref[:, n * width : (n + 1) * width] = piece[...]


def shifted(tail, head):
    n = lax.axis_size("tm")
    left = lax.ppermute(tail, "tm", [(i, i + 1) for i in range(n - 1)])
    right = lax.ppermute(head, "tm", [(i + 1, i) for i in range(n - 1)])
    return left, right


def local(frames, cotangent, routes, lengths, conv_weight, norm_gain, expert_in, expert_out):
    count, width = frames.shape[1:]
    kernel = conv_weight.shape[0]
    chunks = width // LANES
    devices = lax.axis_size("rec") * lax.axis_size("tm")
    hidden = expert_in.shape[2]
    rows = devices * SLOTS
    x, cot = hbm(frames[0]), hbm(cotangent[0])
    win, wout = hbm(expert_in[0]), hbm(expert_out[0])
    place = lax.axis_index("tm")
    scalars = jnp.stack([lengths[0] - place * count, place % 2])
    row = hbm(routes[0].reshape(1, count))
    conv_weight, norm_gain = hbm(conv_weight), hbm(norm_gain)
    shape = jax.ShapeDtypeStruct
    wide = shape((chunks, count, LANES), jnp.float32)
    padded = shape((chunks, count + 2 * EDGE, LANES), jnp.float32)
    lane = shape((count, LANES), jnp.float32)
    buffer = shape((2 * rows, width), jnp.bfloat16)
    half = shape(((kernel + 1) // 2, width), jnp.float32)
    left, right = shifted(frames[0, count - EDGE :], frames[0, :EDGE])
    conv, pad, squares, pick, grads, taps = pl.pallas_call(
        pre_kernel,
        out_shape=[
            wide, padded, lane, shape((2 * rows, count), jnp.bfloat16), buffer,
            shape((chunks, 32, LANES), jnp.float32),
        ],
        in_specs=[SMEM] + [HBM] * 5,
        out_specs=[VMEM] * 6,
        scratch_shapes=[
            pltpu.VMEM((1, count), jnp.int32),
            pltpu.VMEM((count, width), jnp.bfloat16),
            pltpu.VMEM((count, width), jnp.bfloat16),
            pltpu.VMEM((kernel, width), jnp.float32),
            pltpu.VMEM((width,), jnp.float32),
            pltpu.VMEM((count, width), jnp.bfloat16),
            pltpu.SemaphoreType.DMA((5,)),
        ],
        compiler_params=limit(20),
        cost_estimate=cost(6 * 10**9, 2 * 10**7),
        name="pre",
    )(scalars, row, x, cot, conv_weight, norm_gain)
    conv, pad, send, inv = pl.pallas_call(
        send_kernel,
        out_shape=[wide, padded, buffer, lane],
        in_specs=[SMEM] + [VMEM] * 8,
        out_specs=[VMEM] * 4,
        scratch_shapes=[
            pltpu.VMEM((count, width), jnp.bfloat16),
            pltpu.VMEM((count, LANES), jnp.float32),
        ],
        compiler_params=limit(20),
        cost_estimate=cost(10**9, 10**7),
        name="send",
    )(scalars, left, right, conv, pad, squares, pick, grads, taps)
    recv = lax.all_to_all(send, ("rec", "tm"), split_axis=0, concat_axis=0, tiled=True)
    wide_rows = shape((rows, hidden), jnp.bfloat16)
    back, act, d_pre = pl.pallas_call(
        expert_kernel,
        out_shape=[pltpu.HBM(v.shape, v.dtype) for v in (buffer, wide_rows, wide_rows)],
        in_specs=[HBM] * 3,
        out_specs=[HBM] * 3,
        scratch_shapes=[
            pltpu.VMEM((2 * rows, width), jnp.bfloat16),
            pltpu.VMEM((width, hidden), jnp.bfloat16),
            pltpu.VMEM((hidden, width), jnp.bfloat16),
            pltpu.VMEM((rows, width), jnp.bfloat16),
            pltpu.VMEM((rows, width), jnp.bfloat16),
            pltpu.VMEM((rows, hidden), jnp.bfloat16),
            pltpu.VMEM((rows, hidden), jnp.bfloat16),
            pltpu.VMEM((rows, width), jnp.float32),
            pltpu.VMEM((rows, width), jnp.float32),
            pltpu.SemaphoreType.DMA((2, rows // 128)),
            pltpu.SemaphoreType.DMA((2, hidden // TILE)),
            pltpu.SemaphoreType.DMA((2, hidden // TILE)),
        ],
        compiler_params=limit(40),
        cost_estimate=cost(8 * rows * width * hidden, 2 * 10**7),
        name="experts",
    )(hbm(recv), win, wout)
    home = lax.all_to_all(back, ("rec", "tm"), split_axis=0, concat_axis=0, tiled=True)
    grad_in, grad_out, done = pl.pallas_call(
        grads_kernel,
        grid=(hidden // TILE,),
        out_shape=[
            shape((1, width, hidden), jnp.bfloat16),
            shape((1, hidden, width), jnp.bfloat16),
            shape((8, LANES), jnp.float32),
        ],
        in_specs=[
            pl.BlockSpec((2 * rows, width), lambda i: (0, 0)),
            pl.BlockSpec((rows, TILE), lambda i: (0, i)),
            pl.BlockSpec((rows, TILE), lambda i: (0, i)),
        ],
        out_specs=[
            pl.BlockSpec((1, width, TILE), lambda i: (0, 0, i)),
            pl.BlockSpec((1, TILE, width), lambda i: (0, i, 0)),
            pl.BlockSpec((8, LANES), lambda i: (0, 0)),
        ],
        scratch_shapes=[
            pltpu.VMEM((rows, width), jnp.bfloat16),
            pltpu.VMEM((rows, width), jnp.bfloat16),
        ],
        compiler_params=limit(24),
        cost_estimate=cost(4 * rows * width * hidden, 2 * 10**7),
        name="weight_grads",
    )(hbm(recv), hbm(act), hbm(d_pre))
    edges = shape((chunks, EDGE, LANES), jnp.float32)
    output, d_conv, head, tail, mine, other = pl.pallas_call(
        post_kernel,
        out_shape=[shape((count, width), jnp.bfloat16), wide, edges, edges, half, half],
        in_specs=[SMEM] + [HBM] * 7 + [ANY],
        out_specs=[VMEM] * 6,
        scratch_shapes=[
            pltpu.VMEM((1, count), jnp.int32),
            pltpu.VMEM((2 * rows, width), jnp.bfloat16),
            pltpu.VMEM((count, width), jnp.bfloat16),
            pltpu.VMEM((count, LANES), jnp.float32),
            pltpu.VMEM(wide.shape, jnp.float32),
            pltpu.VMEM((chunks, 32, LANES), jnp.float32),
            pltpu.VMEM(padded.shape, jnp.float32),
            pltpu.VMEM((count, width), jnp.float32),
            pltpu.VMEM((count, width), jnp.float32),
            pltpu.VMEM((count, LANES), jnp.float32),
            pltpu.VMEM((kernel + 1, width), jnp.float32),
            pltpu.SemaphoreType.DMA((7,)),
        ],
        compiler_params=limit(24),
        cost_estimate=cost(10**9, 10**7),
        name="post",
    )(scalars, row, hbm(home), cot, hbm(inv), hbm(conv), hbm(taps), hbm(pad), done)
    left, right = shifted(tail, head)

    def back_part(first, tie):
        return pl.pallas_call(
            functools.partial(back_kernel, first),
            out_shape=shape((count, 2 * LANES), jnp.bfloat16),
            in_specs=[SMEM] + [VMEM] * 4 + [ANY],
            out_specs=VMEM,
            scratch_shapes=[
                pltpu.VMEM((2, ROWS + 2 * EDGE, LANES), jnp.float32),
                pltpu.VMEM((2, ROWS + 2 * EDGE, LANES), jnp.float32),
            ],
            compiler_params=limit(8),
            cost_estimate=cost(10**9, 4 * 10**6),
            name="conv_back",
        )(scalars, d_conv, left, right, taps, tie)

    def add(part, others, tie):
        return pl.pallas_call(
            add_kernel,
            out_shape=half,
            in_specs=[ANY] + [VMEM] * 4,
            out_specs=VMEM,
            compiler_params=limit(4),
            name="ring_add",
        )(tie, part, *others)

    n_rec, n_tm = lax.axis_size("rec"), lax.axis_size("tm")
    swap = [(i, i ^ 1) for i in range(n_tm)]
    part = mine + lax.ppermute(other, "tm", swap)
    pieces = []
    for axis, size, step in (("tm", n_tm, 2), ("rec", n_rec, 1), ("tm", n_tm, 8)):
        others = [
            lax.ppermute(part, axis, [(i, i ^ (step * flip)) for i in range(size)])
            for flip in (1, 2, 3)
        ]
        pieces.append(back_part(2 * len(pieces), part))
        part = add(part, others, pieces[-1])
    fellow = lax.ppermute(part, "tm", swap)
    grad_conv, grad_gain, grad_frames = pl.pallas_call(
        functools.partial(finish_kernel, 1.0 / math.sqrt(n_rec * n_tm * count)),
        out_shape=[
            shape((kernel, width), jnp.float32),
            shape((width,), jnp.float32),
            shape((count, width), jnp.bfloat16),
        ],
        in_specs=[SMEM] + [VMEM] * 5,
        out_specs=[VMEM] * 3,
        compiler_params=limit(8),
        name="finish",
    )(scalars, part, fellow, *pieces)
    return output[None], grad_frames[None], grad_conv, grad_gain, grad_in, grad_out


def solution(mesh):
    placed = (
        P("rec", "tm", None),
        P("rec", "tm", None),
        P("rec", "tm", None),
        P("rec"),
        P(),
        P(),
        P(("rec", "tm"), None, None),
        P(("rec", "tm"), None, None),
    )
    return jax.shard_map(
        local,
        mesh=mesh,
        in_specs=placed,
        out_specs=(
            P("rec", "tm", None),
            P("rec", "tm", None),
            P(),
            P(),
            P(("rec", "tm"), None, None),
            P(("rec", "tm"), None, None),
        ),
        check_vma=False,
    )
```

```python
import functools
import math

import jax
import jax.numpy as jnp
from jax import lax
from jax.experimental import pallas as pl
from jax.experimental.pallas import tpu as pltpu
from jax.sharding import PartitionSpec as P

LANES = 128
EDGE = 16
ROWS = 64
SLOTS = 4
PAIR = 2 * SLOTS
VMEM = pl.BlockSpec(memory_space=pltpu.VMEM)
SMEM = pl.BlockSpec(memory_space=pltpu.SMEM)
ANY = pl.BlockSpec(memory_space=pl.ANY)
HBM = pl.BlockSpec(memory_space=pltpu.HBM)


def f32(x):
    return x.astype(jnp.float32)


def bf16(x):
    return x.astype(jnp.bfloat16)


def dot(a, b, dims=((1,), (0,))):
    return lax.dot_general(a, b, (dims, ((), ())), preferred_element_type=jnp.float32)


def iota(shape, axis):
    return lax.broadcasted_iota(jnp.int32, shape, axis)


def limit(mebibytes):
    return pltpu.CompilerParams(vmem_limit_bytes=mebibytes * 1024 * 1024)


def vmem(x):
    return pltpu.with_memory_space_constraint(x, pltpu.VMEM)


def hbm(x):
    return pltpu.with_memory_space_constraint(x, pltpu.HBM)


def cost(flops, nbytes):
    return pl.CostEstimate(flops=flops, bytes_accessed=nbytes, transcendentals=0)


def pre_kernel(
    nv_ref, row_hbm, x_hbm, cot_hbm, w_hbm, gain_hbm,
    conv_ref, pad_ref, squares_ref, pick_ref, send_ref, taps_ref,
    row_ref, x_ref, cot_ref, w_ref, gain_ref, grads, sems,
):
    count, width = x_ref.shape
    chunks = width // LANES
    kernel = w_ref.shape[0]
    reach = (kernel - 1) // 2
    copies = [
        pltpu.make_async_copy(src, dst, sems.at[i])
        for i, (src, dst) in enumerate(
            (
                (x_hbm, x_ref), (w_hbm, w_ref), (gain_hbm, gain_ref),
                (row_hbm, row_ref), (cot_hbm, cot_ref),
            )
        )
    ]
    for copy in copies:
        copy.start()
    valid = nv_ref[0]
    inside = iota((count, LANES), 0) < valid
    squares_ref[...] = jnp.zeros_like(squares_ref)
    for copy in copies[:3]:
        copy.wait()
    for c in range(chunks):
        lanes = slice(c * LANES, (c + 1) * LANES)
        pad_ref[c, 0:EDGE, :] = jnp.zeros((EDGE, LANES), jnp.float32)
        pad_ref[c, EDGE : EDGE + count, :] = jnp.where(inside, f32(x_ref[:, lanes]), 0.0)
        pad_ref[c, EDGE + count :, :] = jnp.zeros((EDGE, LANES), jnp.float32)
        taps_ref[c, 0:kernel, :] = w_ref[:, lanes]
        taps_ref[c, kernel : kernel + 1, :] = gain_ref[lanes][None, :]

    @pl.loop(0, chunks)
    def _(c):
        for start in range(0, count, ROWS):
            total = jnp.zeros((ROWS, LANES), jnp.float32)
            for k in range(kernel):
                at = start + k + EDGE - reach
                total = total + taps_ref[c, k : k + 1, :] * pad_ref[c, at : at + ROWS, :]
            total = pad_ref[c, EDGE + start : EDGE + start + ROWS, :] + total
            conv_ref[c, start : start + ROWS, :] = total
            if 0 < start < count - ROWS:
                squares_ref[start : start + ROWS, :] += total * total
            else:
                low = EDGE if start == 0 else 0
                high = ROWS if start == 0 else ROWS - EDGE
                inner = total[low:high, :]
                squares_ref[start + low : start + high, :] += inner * inner

    for copy in copies[3:]:
        copy.wait()
    row = row_ref[...]
    experts = send_ref.shape[0] // PAIR
    named = jnp.where(iota((experts, count), 0) == row, 1.0, 0.0)
    before = bf16(jnp.where(iota((count, count), 0) < iota((count, count), 1), 1.0, 0.0))
    slot = jnp.sum(named * dot(bf16(named), before), axis=0, keepdims=True)
    key = row * PAIR + slot.astype(jnp.int32)
    for c in range(chunks):
        lanes = slice(c * LANES, (c + 1) * LANES)
        grads[:, lanes] = bf16(jnp.where(inside, f32(cot_ref[:, lanes]), 0.0))
    block = 256
    for start in range(0, send_ref.shape[0], block):
        seat = iota((block, count), 0) + start
        pick_ref[start : start + block, :] = bf16(jnp.where(seat == key, 1.0, 0.0))
        pick = bf16(jnp.where(seat == key + SLOTS, 1.0, 0.0))
        send_ref[start : start + block, :] = bf16(dot(pick, grads[...]))


def send_kernel(
    nv_ref, left_ref, right_ref, conv_in, pad_in, squares_ref, pick_ref, grads_ref, taps_ref,
    conv_ref, pad_ref, send_ref, inv_ref,
    rows, squares,
):
    chunks, count, _ = conv_in.shape
    width = chunks * LANES
    kernel = taps_ref.shape[1] - 1
    reach = (kernel - 1) // 2
    valid = nv_ref[0]
    edge = iota((EDGE, LANES), 0)
    squares[...] = squares_ref[...]
    for c in range(chunks):
        lanes = slice(c * LANES, (c + 1) * LANES)
        pad_ref[c, 0:EDGE, :] = jnp.where(edge - EDGE < valid, f32(left_ref[:, lanes]), 0.0)
        pad_ref[c, EDGE : EDGE + count, :] = pad_in[c, EDGE : EDGE + count, :]
        pad_ref[c, EDGE + count :, :] = jnp.where(edge + count < valid, f32(right_ref[:, lanes]), 0.0)
        conv_ref[c, EDGE : count - EDGE, :] = conv_in[c, EDGE : count - EDGE, :]
        for start in (0, count - EDGE):
            total = jnp.zeros((EDGE, LANES), jnp.float32)
            for k in range(kernel):
                at = start + k + EDGE - reach
                total = total + taps_ref[c, k : k + 1, :] * pad_ref[c, at : at + EDGE, :]
            total = pad_ref[c, EDGE + start : EDGE + start + EDGE, :] + total
            conv_ref[c, start : start + EDGE, :] = total
            squares[start : start + EDGE, :] += total * total
    inv = lax.rsqrt(jnp.sum(squares[...], axis=-1, keepdims=True) * (1.0 / width) + 1e-05)
    inv = jnp.broadcast_to(inv, (count, LANES))
    inv_ref[...] = inv
    for c in range(chunks):
        lanes = slice(c * LANES, (c + 1) * LANES)
        rows[:, lanes] = bf16(conv_ref[c] * inv * taps_ref[c, kernel : kernel + 1, :])
    block = 256
    for start in range(0, send_ref.shape[0], block):
        part = slice(start, start + block)
        send_ref[part, :] = bf16(dot(pick_ref[part, :], rows[...]) + f32(grads_ref[part, :]))


def picks():
    half, whole = 128, 256
    i, r = iota((half, whole), 0), iota((half, whole), 1)
    place = (i // SLOTS) * PAIR + i % SLOTS
    return bf16(jnp.where(r == place, 1.0, 0.0)), bf16(jnp.where(r == place + SLOTS, 1.0, 0.0))


def unpack(recv_ref, x_ref, g_ref):
    pick_x, pick_g = picks()
    half, whole = pick_x.shape
    for n in range(x_ref.shape[0] // half):
        part = recv_ref[n * whole : (n + 1) * whole, :]
        x_ref[n * half : (n + 1) * half, :] = bf16(dot(pick_x, part))
        g_ref[n * half : (n + 1) * half, :] = bf16(dot(pick_g, part))


def pack(rows, put, n):
    half = put[0].shape[1]
    part = bf16(rows[n * half : (n + 1) * half, :])
    cut = part.shape[1] // 2
    return bf16(dot(put[0], part[:, :cut]) + dot(put[1], part[:, cut:]))


def puts():
    half, whole = 128, 256
    q, j = iota((whole, half), 0), iota((whole, half), 1)
    home = (j // SLOTS) * PAIR + j % SLOTS
    return bf16(jnp.where(q == home, 1.0, 0.0)), bf16(jnp.where(q == home + SLOTS, 1.0, 0.0))


TILE = 512


def expert_kernel(
    recv_ref, win_ref, wout_ref,
    back_hbm, x_hbm, g_hbm, act_hbm, dpre_hbm,
    x_ref, g_ref, act_ref, dpre_ref, d_rows, back_ref, row_sems, back_sems, out_sems,
):
    rows = x_ref.shape[0]
    hidden = win_ref.shape[1]
    tiles = hidden // TILE
    half, whole = 128, 256
    groups = rows // half
    returns, stores = [], []
    for n in range(groups):
        part = pl.ds(n * whole, whole)
        returns.append(pltpu.make_async_copy(back_ref.at[part, :], back_hbm.at[part, :], back_sems.at[n]))
    for n in range(tiles):
        cols = pl.ds(n * TILE, TILE)
        stores.append((
            pltpu.make_async_copy(act_ref.at[:, cols], act_hbm.at[:, cols], out_sems.at[0, n]),
            pltpu.make_async_copy(dpre_ref.at[:, cols], dpre_hbm.at[:, cols], out_sems.at[1, n]),
        ))
    unpack(recv_ref, x_ref, g_ref)
    stores.append((
        pltpu.make_async_copy(x_ref, x_hbm, row_sems.at[0]),
        pltpu.make_async_copy(g_ref, g_hbm, row_sems.at[1]),
    ))
    for copy in stores[tiles]:
        copy.start()

    def front(n):
        cols = slice(n * TILE, (n + 1) * TILE)
        return (
            dot(x_ref[...], win_ref[:, cols]),
            dot(g_ref[...], wout_ref[cols, :], ((1,), (1,))),
        )

    ready = front(0)
    for n in range(tiles):
        cols = slice(n * TILE, (n + 1) * TILE)
        pre, d_act = ready
        if n + 1 < tiles:
            ready = front(n + 1)
        gate = 0.5 * jnp.tanh(0.5 * pre) + 0.5
        value = pre * gate
        d_pre = bf16(d_act * (gate + value * (1.0 - gate)))
        act_ref[:, cols] = bf16(value)
        dpre_ref[:, cols] = d_pre
        for copy in stores[n]:
            copy.start()
        backward = dot(d_pre, win_ref[:, cols], ((1,), (1,)))
        d_rows[...] = backward + d_rows[...] if n else backward
    put = puts()
    for n in range(groups):
        back_ref[n * whole : (n + 1) * whole, :] = pack(d_rows, put, n)
        returns[n].start()
    for pair in stores:
        for copy in pair:
            copy.wait()
    for copy in returns:
        copy.wait()


def rest_kernel(x_ref, g_ref, act_ref, dpre_ref, wout_ref, gin_ref, gout_ref, back_ref, result):
    n = pl.program_id(0)
    gin_ref[0] = bf16(dot(x_ref[...], dpre_ref[...], ((0,), (0,))))
    gout_ref[0] = bf16(dot(act_ref[...], g_ref[...], ((0,), (0,))))
    forward = dot(act_ref[...], wout_ref[...])

    @pl.when(n == 0)
    def _():
        result[...] = forward

    @pl.when(n > 0)
    def _():
        result[...] += forward

    @pl.when(n == pl.num_programs(0) - 1)
    def _():
        put = puts()
        half, whole = 128, 256
        for m in range(result.shape[0] // half):
            back_ref[m * whole : (m + 1) * whole, :] = pack(result, put, m)


def picked_by(key, seats):
    seat = iota((key.shape[0], seats), 1)
    return bf16(jnp.where(seat == key, 1.0, 0.0)), bf16(jnp.where(seat == key + SLOTS, 1.0, 0.0))


def out_kernel(nv_ref, key_ref, recv_hbm, conv_hbm, tie_ref, out_ref, recv_ref, conv_ref, sems):
    copies = [
        pltpu.make_async_copy(src, dst, sems.at[i])
        for i, (src, dst) in enumerate(((recv_hbm, recv_ref), (conv_hbm, conv_ref)))
    ]
    for copy in copies:
        copy.start()
    count, width = out_ref.shape
    picked = picked_by(key_ref[:, 0:1], recv_ref.shape[0])
    inside = iota((count, LANES), 0) < nv_ref[0]
    for copy in copies:
        copy.wait()
    half = width // 2
    for n in range(2):
        back = dot(picked[n], recv_ref[...])
        for i in range(half // LANES):
            c = n * (half // LANES) + i
            rows = back[:, i * LANES : (i + 1) * LANES]
            out_ref[:, c * LANES : (c + 1) * LANES] = bf16(conv_ref[c] + jnp.where(inside, rows, 0.0))


def post_kernel(
    nv_ref, row_hbm, recv_hbm, cot_hbm, inv_hbm, conv_hbm, taps_hbm, pad_hbm, tie_ref,
    dconv_ref, head_ref, tail_ref, mine_ref, other_ref, key_ref,
    row_ref, recv_ref, cot_ref, inv_ref, conv_ref, taps_ref, pad_ref,
    dhid, means, sums_ref, sems,
):
    copies = [
        pltpu.make_async_copy(src, dst, sems.at[i])
        for i, (src, dst) in enumerate(
            (
                (row_hbm, row_ref), (recv_hbm, recv_ref), (cot_hbm, cot_ref), (inv_hbm, inv_ref),
                (conv_hbm, conv_ref), (taps_hbm, taps_ref), (pad_hbm, pad_ref),
            )
        )
    ]
    for copy in copies:
        copy.start()
    count, width = cot_ref.shape
    chunks = width // LANES
    kernel = sums_ref.shape[0] - 1
    reach = (kernel - 1) // 2
    copies[0].wait()
    row = row_ref[...]
    here, there = iota((count, count), 0), iota((count, count), 1)
    col = jnp.sum(jnp.where(here == there, f32(row), 0.0), axis=1, keepdims=True).astype(jnp.int32)
    earlier = (col == row) & (there < here)
    slot = jnp.sum(jnp.where(earlier, 1.0, 0.0), axis=1, keepdims=True).astype(jnp.int32)
    key = col * PAIR + slot
    key_ref[...] = jnp.broadcast_to(key, key_ref.shape)
    picked = picked_by(key, recv_ref.shape[0])
    copies[1].wait()
    for n in range(2):
        dhid[:, n * (width // 2) : (n + 1) * (width // 2)] = dot(picked[n], recv_ref[...])
    for copy in copies[2:]:
        copy.wait()
    inv = inv_ref[...]
    means[...] = jnp.zeros_like(means)
    for c in range(chunks):
        lanes = slice(c * LANES, (c + 1) * LANES)
        normed = conv_ref[c] * inv
        d_hidden = dhid[:, lanes]
        means[...] += d_hidden * taps_ref[c, kernel : kernel + 1, :] * normed
        sums_ref[kernel : kernel + 1, lanes] = jnp.sum(d_hidden * normed, axis=0, keepdims=True)
    mean = jnp.sum(means[...], axis=-1, keepdims=True) * (1.0 / width)
    mean = jnp.broadcast_to(mean, (count, LANES))
    for c in range(chunks):
        lanes = slice(c * LANES, (c + 1) * LANES)
        d_conv = f32(cot_ref[:, lanes]) + inv * (
            dhid[:, lanes] * taps_ref[c, kernel : kernel + 1, :] - conv_ref[c] * inv * mean
        )
        dconv_ref[c] = d_conv
        head_ref[c] = d_conv[0:EDGE, :]
        tail_ref[c] = d_conv[count - EDGE :, :]
    for c in range(chunks):
        lanes = slice(c * LANES, (c + 1) * LANES)
        totals = [jnp.zeros((8, LANES), jnp.float32) for _ in range(kernel)]
        for start in range(0, count, ROWS):
            part = dconv_ref[c, start : start + ROWS, :]
            for k in range(kernel):
                at = start + k + EDGE - reach
                product = part * pad_ref[c, at : at + ROWS, :]
                totals[k] = totals[k] + jnp.sum(product.reshape(ROWS // 8, 8, LANES), axis=0)
        for k in range(kernel):
            sums_ref[k : k + 1, lanes] = jnp.sum(totals[k], axis=0, keepdims=True)
    core = nv_ref[1]
    rows = mine_ref.shape[0]
    low, high = sums_ref[0:rows, :], sums_ref[rows:, :]
    mine_ref[...] = jnp.where(core == 0, low, high)
    other_ref[...] = jnp.where(core == 0, high, low)


def back_kernel(first, nv_ref, dconv_ref, left_ref, right_ref, taps_ref, tie_ref, grad_ref, low, high):
    _, count, _ = dconv_ref.shape
    kernel = taps_ref.shape[1] - 1
    reach = (kernel - 1) // 2
    valid = nv_ref[0]
    for i in range(grad_ref.shape[1] // LANES):
        c = first + i
        lanes = slice(i * LANES, (i + 1) * LANES)
        low[i, 0:EDGE, :] = left_ref[c]
        low[i, EDGE:, :] = dconv_ref[c, 0 : ROWS + EDGE, :]
        high[i, 0 : ROWS + EDGE, :] = dconv_ref[c, count - ROWS - EDGE :, :]
        high[i, ROWS + EDGE :, :] = right_ref[c]
        for start in range(0, count, ROWS):
            if start == 0:
                window, shift, at = low, EDGE, i
            elif start == count - ROWS:
                window, shift, at = high, EDGE - start, i
            else:
                window, shift, at = dconv_ref, 0, c
            total = jnp.zeros((ROWS, LANES), jnp.float32)
            for k in range(kernel):
                begin = start + shift + reach - k
                total = total + taps_ref[c, k : k + 1, :] * window[at, begin : begin + ROWS, :]
            total = window[at, start + shift : start + shift + ROWS, :] + total
            keep = iota((ROWS, LANES), 0) + start < valid
            grad_ref[start : start + ROWS, lanes] = bf16(jnp.where(keep, total, 0.0))


def add_kernel(own_ref, one_ref, two_ref, three_ref, *refs):
    out_ref = refs[-1]
    out_ref[...] = (own_ref[...] + one_ref[...]) + (two_ref[...] + three_ref[...])


def finish_kernel(scale, nv_ref, part_ref, fellow_ref, *refs):
    pieces, (taps_ref, gain_ref, grad_ref) = refs[:-3], refs[-3:]
    core = nv_ref[1]
    rows = part_ref.shape[0]
    part, fellow = part_ref[...] * scale, fellow_ref[...] * scale
    low = jnp.where(core == 0, part, fellow)
    high = jnp.where(core == 0, fellow, part)
    taps_ref[0:rows, :] = low
    taps_ref[rows:, :] = high[0 : rows - 1, :]
    gain_ref[...] = high[rows - 1, :]
    width = pieces[0].shape[1]
    for n, piece in enumerate(pieces):
        grad_ref[:, n * width : (n + 1) * width] = piece[...]


def shifted(tail, head):
    n = lax.axis_size("tm")
    left = lax.ppermute(tail, "tm", [(i, i + 1) for i in range(n - 1)])
    right = lax.ppermute(head, "tm", [(i + 1, i) for i in range(n - 1)])
    return left, right


def local(frames, cotangent, routes, lengths, conv_weight, norm_gain, expert_in, expert_out):
    count, width = frames.shape[1:]
    kernel = conv_weight.shape[0]
    chunks = width // LANES
    devices = lax.axis_size("rec") * lax.axis_size("tm")
    hidden = expert_in.shape[2]
    rows = devices * SLOTS
    x, cot = hbm(frames[0]), hbm(cotangent[0])
    win, wout = hbm(expert_in[0]), hbm(expert_out[0])
    place = lax.axis_index("tm")
    scalars = jnp.stack([lengths[0] - place * count, place % 2])
    row = hbm(routes[0].reshape(1, count))
    conv_weight, norm_gain = hbm(conv_weight), hbm(norm_gain)
    shape = jax.ShapeDtypeStruct
    wide = shape((chunks, count, LANES), jnp.float32)
    padded = shape((chunks, count + 2 * EDGE, LANES), jnp.float32)
    lane = shape((count, LANES), jnp.float32)
    buffer = shape((2 * rows, width), jnp.bfloat16)
    half = shape(((kernel + 1) // 2, width), jnp.float32)
    left, right = shifted(frames[0, count - EDGE :], frames[0, :EDGE])
    conv, pad, squares, pick, grads, taps = pl.pallas_call(
        pre_kernel,
        out_shape=[
            wide, padded, lane, shape((2 * rows, count), jnp.bfloat16), buffer,
            shape((chunks, 32, LANES), jnp.float32),
        ],
        in_specs=[SMEM] + [HBM] * 5,
        out_specs=[VMEM] * 6,
        scratch_shapes=[
            pltpu.VMEM((1, count), jnp.int32),
            pltpu.VMEM((count, width), jnp.bfloat16),
            pltpu.VMEM((count, width), jnp.bfloat16),
            pltpu.VMEM((kernel, width), jnp.float32),
            pltpu.VMEM((width,), jnp.float32),
            pltpu.VMEM((count, width), jnp.bfloat16),
            pltpu.SemaphoreType.DMA((5,)),
        ],
        compiler_params=limit(20),
        cost_estimate=cost(6 * 10**9, 2 * 10**7),
        name="pre",
    )(scalars, row, x, cot, conv_weight, norm_gain)
    conv, pad, send, inv = pl.pallas_call(
        send_kernel,
        out_shape=[wide, padded, buffer, lane],
        in_specs=[SMEM] + [VMEM] * 8,
        out_specs=[VMEM] * 4,
        scratch_shapes=[
            pltpu.VMEM((count, width), jnp.bfloat16),
            pltpu.VMEM((count, LANES), jnp.float32),
        ],
        compiler_params=limit(20),
        cost_estimate=cost(10**9, 10**7),
        name="send",
    )(scalars, left, right, conv, pad, squares, pick, grads, taps)
    recv = lax.all_to_all(send, ("rec", "tm"), split_axis=0, concat_axis=0, tiled=True)
    wide_rows = shape((rows, hidden), jnp.bfloat16)
    these = shape((rows, width), jnp.bfloat16)
    halves = shape((2 * rows, width // 2), jnp.bfloat16)
    tiles = hidden // TILE
    back, rows_x, rows_g, act, d_pre = pl.pallas_call(
        expert_kernel,
        out_shape=[pltpu.HBM(v.shape, v.dtype) for v in (halves, these, these, wide_rows, wide_rows)],
        in_specs=[VMEM] * 3,
        out_specs=[HBM] * 5,
        scratch_shapes=[
            pltpu.VMEM((rows, width), jnp.bfloat16),
            pltpu.VMEM((rows, width), jnp.bfloat16),
            pltpu.VMEM((rows, hidden), jnp.bfloat16),
            pltpu.VMEM((rows, hidden), jnp.bfloat16),
            pltpu.VMEM((rows, width), jnp.float32),
            pltpu.VMEM((2 * rows, width // 2), jnp.bfloat16),
            pltpu.SemaphoreType.DMA((2,)),
            pltpu.SemaphoreType.DMA((rows // 128,)),
            pltpu.SemaphoreType.DMA((2, tiles)),
        ],
        compiler_params=limit(30),
        cost_estimate=cost(6 * rows * width * hidden, 2 * 10**7),
        name="experts",
    )(recv, vmem(expert_in[0]), vmem(expert_out[0]))
    home = lax.all_to_all(back, ("rec", "tm"), split_axis=0, concat_axis=0, tiled=True)
    grad_in, grad_out, back = pl.pallas_call(
        rest_kernel,
        grid=(tiles,),
        out_shape=[
            shape((1, width, hidden), jnp.bfloat16),
            shape((1, hidden, width), jnp.bfloat16),
            pltpu.HBM(halves.shape, halves.dtype),
        ],
        in_specs=[
            pl.BlockSpec((rows, width), lambda i: (0, 0)),
            pl.BlockSpec((rows, width), lambda i: (0, 0)),
            pl.BlockSpec((rows, TILE), lambda i: (0, i)),
            pl.BlockSpec((rows, TILE), lambda i: (0, i)),
            pl.BlockSpec((TILE, width), lambda i: (i, 0)),
        ],
        out_specs=[
            pl.BlockSpec((1, width, TILE), lambda i: (0, 0, i)),
            pl.BlockSpec((1, TILE, width), lambda i: (0, i, 0)),
            pl.BlockSpec((2 * rows, width // 2), lambda i: (0, 0)),
        ],
        scratch_shapes=[pltpu.VMEM((rows, width), jnp.float32)],
        compiler_params=limit(24),
        cost_estimate=cost(6 * rows * width * hidden, 2 * 10**7),
        name="weight_grads",
    )(hbm(rows_x), hbm(rows_g), hbm(act), hbm(d_pre), wout)
    home_out = lax.all_to_all(back, ("rec", "tm"), split_axis=0, concat_axis=0, tiled=True)
    edges = shape((chunks, EDGE, LANES), jnp.float32)
    d_conv, head, tail, mine, other, key = pl.pallas_call(
        post_kernel,
        out_shape=[wide, edges, edges, half, half, shape((count, LANES), jnp.int32)],
        in_specs=[SMEM] + [HBM] * 7 + [ANY],
        out_specs=[VMEM] * 6,
        scratch_shapes=[
            pltpu.VMEM((1, count), jnp.int32),
            pltpu.VMEM((2 * rows, width // 2), jnp.bfloat16),
            pltpu.VMEM((count, width), jnp.bfloat16),
            pltpu.VMEM((count, LANES), jnp.float32),
            pltpu.VMEM(wide.shape, jnp.float32),
            pltpu.VMEM((chunks, 32, LANES), jnp.float32),
            pltpu.VMEM(padded.shape, jnp.float32),
            pltpu.VMEM((count, width), jnp.float32),
            pltpu.VMEM((count, LANES), jnp.float32),
            pltpu.VMEM((kernel + 1, width), jnp.float32),
            pltpu.SemaphoreType.DMA((7,)),
        ],
        compiler_params=limit(24),
        cost_estimate=cost(10**9, 10**7),
        name="post",
    )(scalars, row, home, cot, hbm(inv), hbm(conv), hbm(taps), hbm(pad), hbm(back))
    left, right = shifted(tail, head)

    def back_part(first, tie):
        return pl.pallas_call(
            functools.partial(back_kernel, first),
            out_shape=shape((count, 2 * LANES), jnp.bfloat16),
            in_specs=[SMEM] + [VMEM] * 4 + [ANY],
            out_specs=VMEM,
            scratch_shapes=[
                pltpu.VMEM((2, ROWS + 2 * EDGE, LANES), jnp.float32),
                pltpu.VMEM((2, ROWS + 2 * EDGE, LANES), jnp.float32),
            ],
            compiler_params=limit(8),
            cost_estimate=cost(10**9, 4 * 10**6),
            name="conv_back",
        )(scalars, d_conv, left, right, taps, tie)

    def add(part, others, ties):
        return pl.pallas_call(
            add_kernel,
            out_shape=half,
            in_specs=[VMEM] * 4 + [ANY] * len(ties),
            out_specs=VMEM,
            compiler_params=limit(4),
            name="ring_add",
        )(part, *others, *ties)

    n_rec, n_tm = lax.axis_size("rec"), lax.axis_size("tm")
    swap = [(i, i ^ 1) for i in range(n_tm)]
    part = mine + lax.ppermute(other, "tm", swap)
    def out(tie):
        return pl.pallas_call(
            out_kernel,
            out_shape=shape((count, width), jnp.bfloat16),
            in_specs=[SMEM, VMEM] + [HBM] * 2 + [ANY],
            out_specs=VMEM,
            scratch_shapes=[
                pltpu.VMEM((2 * rows, width // 2), jnp.bfloat16),
                pltpu.VMEM(wide.shape, jnp.float32),
                pltpu.SemaphoreType.DMA((2,)),
            ],
            compiler_params=limit(16),
            cost_estimate=cost(10**9, 4 * 10**6),
            name="out",
        )(scalars, key, home_out, hbm(conv), tie)

    beside = (
        lambda tie: [],
        lambda tie: [back_part(0, tie), back_part(2, tie), back_part(4, tie)],
        lambda tie: [out(tie)],
    )
    done = []
    for (axis, size, step), work in zip((("tm", n_tm, 2), ("rec", n_rec, 1), ("tm", n_tm, 8)), beside):
        others = [
            lax.ppermute(part, axis, [(i, i ^ (step * flip)) for i in range(size)])
            for flip in (1, 2, 3)
        ]
        ties = work(part)
        done += ties
        part = add(part, others, ties if len(done) <= 3 else [hbm(done[3])])
    *pieces, output = done
    fellow = lax.ppermute(part, "tm", swap)
    grad_conv, grad_gain, grad_frames = pl.pallas_call(
        functools.partial(finish_kernel, 1.0 / math.sqrt(n_rec * n_tm * count)),
        out_shape=[
            shape((kernel, width), jnp.float32),
            shape((width,), jnp.float32),
            shape((count, width), jnp.bfloat16),
        ],
        in_specs=[SMEM] + [VMEM] * 5,
        out_specs=[VMEM] * 3,
        compiler_params=limit(8),
        name="finish",
    )(scalars, part, fellow, *pieces)
    return output[None], grad_frames[None], grad_conv, grad_gain, grad_in, grad_out


def solution(mesh):
    placed = (
        P("rec", "tm", None),
        P("rec", "tm", None),
        P("rec", "tm", None),
        P("rec"),
        P(),
        P(),
        P(("rec", "tm"), None, None),
        P(("rec", "tm"), None, None),
    )
    return jax.shard_map(
        local,
        mesh=mesh,
        in_specs=placed,
        out_specs=(
            P("rec", "tm", None),
            P("rec", "tm", None),
            P(),
            P(),
            P(("rec", "tm"), None, None),
            P(("rec", "tm"), None, None),
        ),
        check_vma=False,
    )
```

```python
import functools
import math

import jax
import jax.numpy as jnp
from jax import lax
from jax.experimental import pallas as pl
from jax.experimental.pallas import tpu as pltpu
from jax.sharding import PartitionSpec as P

LANES = 128
EDGE = 16
ROWS = 64
SLOTS = 4
PAIR = 2 * SLOTS
VMEM = pl.BlockSpec(memory_space=pltpu.VMEM)
SMEM = pl.BlockSpec(memory_space=pltpu.SMEM)
ANY = pl.BlockSpec(memory_space=pl.ANY)
HBM = pl.BlockSpec(memory_space=pltpu.HBM)


def f32(x):
    return x.astype(jnp.float32)


def bf16(x):
    return x.astype(jnp.bfloat16)


def dot(a, b, dims=((1,), (0,))):
    return lax.dot_general(a, b, (dims, ((), ())), preferred_element_type=jnp.float32)


def iota(shape, axis):
    return lax.broadcasted_iota(jnp.int32, shape, axis)


def limit(mebibytes):
    return pltpu.CompilerParams(vmem_limit_bytes=mebibytes * 1024 * 1024)


def vmem(x):
    return pltpu.with_memory_space_constraint(x, pltpu.VMEM)


def hbm(x):
    return pltpu.with_memory_space_constraint(x, pltpu.HBM)


def cost(flops, nbytes):
    return pl.CostEstimate(flops=flops, bytes_accessed=nbytes, transcendentals=0)


def pre_kernel(
    nv_ref, row_hbm, x_hbm, cot_hbm, w_hbm, gain_hbm,
    conv_ref, pad_ref, squares_ref, pick_ref, send_ref, taps_ref, first_ref, last_ref,
    row_ref, x_ref, cot_ref, w_ref, gain_ref, grads, sems,
):
    count, width = x_ref.shape
    chunks = width // LANES
    kernel = w_ref.shape[0]
    reach = (kernel - 1) // 2
    copies = [
        pltpu.make_async_copy(src, dst, sems.at[i])
        for i, (src, dst) in enumerate(
            (
                (x_hbm, x_ref), (w_hbm, w_ref), (gain_hbm, gain_ref),
                (row_hbm, row_ref), (cot_hbm, cot_ref),
            )
        )
    ]
    for copy in copies:
        copy.start()
    valid = nv_ref[0]
    inside = iota((count, LANES), 0) < valid
    squares_ref[...] = jnp.zeros_like(squares_ref)
    for copy in copies[:3]:
        copy.wait()
    first_ref[...] = x_ref[0:EDGE, :]
    last_ref[...] = x_ref[count - EDGE :, :]
    for c in range(chunks):
        lanes = slice(c * LANES, (c + 1) * LANES)
        pad_ref[c, 0:EDGE, :] = jnp.zeros((EDGE, LANES), jnp.float32)
        pad_ref[c, EDGE : EDGE + count, :] = jnp.where(inside, f32(x_ref[:, lanes]), 0.0)
        pad_ref[c, EDGE + count :, :] = jnp.zeros((EDGE, LANES), jnp.float32)
        taps_ref[c, 0:kernel, :] = w_ref[:, lanes]
        taps_ref[c, kernel : kernel + 1, :] = gain_ref[lanes][None, :]

    @pl.loop(0, chunks)
    def _(c):
        for start in range(0, count, ROWS):
            total = jnp.zeros((ROWS, LANES), jnp.float32)
            for k in range(kernel):
                at = start + k + EDGE - reach
                total = total + taps_ref[c, k : k + 1, :] * pad_ref[c, at : at + ROWS, :]
            total = pad_ref[c, EDGE + start : EDGE + start + ROWS, :] + total
            conv_ref[c, start : start + ROWS, :] = total
            if 0 < start < count - ROWS:
                squares_ref[start : start + ROWS, :] += total * total
            else:
                low = EDGE if start == 0 else 0
                high = ROWS if start == 0 else ROWS - EDGE
                inner = total[low:high, :]
                squares_ref[start + low : start + high, :] += inner * inner

    for copy in copies[3:]:
        copy.wait()
    row = row_ref[...]
    experts = send_ref.shape[0] // PAIR
    named = jnp.where(iota((experts, count), 0) == row, 1.0, 0.0)
    before = bf16(jnp.where(iota((count, count), 0) < iota((count, count), 1), 1.0, 0.0))
    slot = jnp.sum(named * dot(bf16(named), before), axis=0, keepdims=True)
    key = row * PAIR + slot.astype(jnp.int32)
    for c in range(chunks):
        lanes = slice(c * LANES, (c + 1) * LANES)
        grads[:, lanes] = bf16(jnp.where(inside, f32(cot_ref[:, lanes]), 0.0))
    block = 256
    for start in range(0, send_ref.shape[0], block):
        seat = iota((block, count), 0) + start
        pick_ref[start : start + block, :] = bf16(jnp.where(seat == key, 1.0, 0.0))
        pick = bf16(jnp.where(seat == key + SLOTS, 1.0, 0.0))
        send_ref[start : start + block, :] = bf16(dot(pick, grads[...]))


def send_kernel(
    nv_ref, left_ref, right_ref, conv_in, pad_in, squares_ref, pick_ref, grads_ref, taps_ref,
    conv_ref, pad_ref, send_ref, inv_ref,
    rows, squares,
):
    chunks, count, _ = conv_in.shape
    width = chunks * LANES
    kernel = taps_ref.shape[1] - 1
    reach = (kernel - 1) // 2
    valid = nv_ref[0]
    edge = iota((EDGE, LANES), 0)
    squares[...] = squares_ref[...]
    for c in range(chunks):
        lanes = slice(c * LANES, (c + 1) * LANES)
        pad_ref[c, 0:EDGE, :] = jnp.where(edge - EDGE < valid, f32(left_ref[:, lanes]), 0.0)
        pad_ref[c, EDGE : EDGE + count, :] = pad_in[c, EDGE : EDGE + count, :]
        pad_ref[c, EDGE + count :, :] = jnp.where(edge + count < valid, f32(right_ref[:, lanes]), 0.0)
        conv_ref[c, EDGE : count - EDGE, :] = conv_in[c, EDGE : count - EDGE, :]
        for start in (0, count - EDGE):
            total = jnp.zeros((EDGE, LANES), jnp.float32)
            for k in range(kernel):
                at = start + k + EDGE - reach
                total = total + taps_ref[c, k : k + 1, :] * pad_ref[c, at : at + EDGE, :]
            total = pad_ref[c, EDGE + start : EDGE + start + EDGE, :] + total
            conv_ref[c, start : start + EDGE, :] = total
            squares[start : start + EDGE, :] += total * total
    inv = lax.rsqrt(jnp.sum(squares[...], axis=-1, keepdims=True) * (1.0 / width) + 1e-05)
    inv = jnp.broadcast_to(inv, (count, LANES))
    inv_ref[...] = inv
    for c in range(chunks):
        lanes = slice(c * LANES, (c + 1) * LANES)
        rows[:, lanes] = bf16(conv_ref[c] * inv * taps_ref[c, kernel : kernel + 1, :])
    block = 256
    for start in range(0, send_ref.shape[0], block):
        part = slice(start, start + block)
        send_ref[part, :] = bf16(dot(pick_ref[part, :], rows[...]) + f32(grads_ref[part, :]))


def picks():
    half, whole = 128, 256
    i, r = iota((half, whole), 0), iota((half, whole), 1)
    place = (i // SLOTS) * PAIR + i % SLOTS
    return bf16(jnp.where(r == place, 1.0, 0.0)), bf16(jnp.where(r == place + SLOTS, 1.0, 0.0))


def unpack(recv_ref, x_ref, g_ref):
    pick_x, pick_g = picks()
    half, whole = pick_x.shape
    for n in range(x_ref.shape[0] // half):
        part = recv_ref[n * whole : (n + 1) * whole, :]
        x_ref[n * half : (n + 1) * half, :] = bf16(dot(pick_x, part))
        g_ref[n * half : (n + 1) * half, :] = bf16(dot(pick_g, part))


def pack(rows, put, n):
    half = put[0].shape[1]
    part = bf16(rows[n * half : (n + 1) * half, :])
    cut = part.shape[1] // 2
    return bf16(dot(put[0], part[:, :cut]) + dot(put[1], part[:, cut:]))


def puts():
    half, whole = 128, 256
    q, j = iota((whole, half), 0), iota((whole, half), 1)
    home = (j // SLOTS) * PAIR + j % SLOTS
    return bf16(jnp.where(q == home, 1.0, 0.0)), bf16(jnp.where(q == home + SLOTS, 1.0, 0.0))


TILE = 512


def expert_kernel(
    recv_ref, win_ref, wout_ref,
    back_hbm, x_hbm, g_hbm, act_hbm, dpre_hbm,
    x_ref, g_ref, act_ref, dpre_ref, d_rows, back_ref, row_sems, back_sems, out_sems,
):
    rows = x_ref.shape[0]
    hidden = win_ref.shape[1]
    tiles = hidden // TILE
    half, whole = 128, 256
    groups = rows // half
    returns, stores = [], []
    for n in range(groups):
        part = pl.ds(n * whole, whole)
        returns.append(pltpu.make_async_copy(back_ref.at[part, :], back_hbm.at[part, :], back_sems.at[n]))
    for n in range(tiles):
        cols = pl.ds(n * TILE, TILE)
        stores.append((
            pltpu.make_async_copy(act_ref.at[:, cols], act_hbm.at[:, cols], out_sems.at[0, n]),
            pltpu.make_async_copy(dpre_ref.at[:, cols], dpre_hbm.at[:, cols], out_sems.at[1, n]),
        ))
    unpack(recv_ref, x_ref, g_ref)
    stores.append((
        pltpu.make_async_copy(x_ref, x_hbm, row_sems.at[0]),
        pltpu.make_async_copy(g_ref, g_hbm, row_sems.at[1]),
    ))
    for copy in stores[tiles]:
        copy.start()

    def front(n):
        cols = slice(n * TILE, (n + 1) * TILE)
        return (
            dot(x_ref[...], win_ref[:, cols]),
            dot(g_ref[...], wout_ref[cols, :], ((1,), (1,))),
        )

    ready = front(0)
    for n in range(tiles):
        cols = slice(n * TILE, (n + 1) * TILE)
        pre, d_act = ready
        if n + 1 < tiles:
            ready = front(n + 1)
        gate = 0.5 * jnp.tanh(0.5 * pre) + 0.5
        value = pre * gate
        d_pre = bf16(d_act * (gate + value * (1.0 - gate)))
        act_ref[:, cols] = bf16(value)
        dpre_ref[:, cols] = d_pre
        for copy in stores[n]:
            copy.start()
        backward = dot(d_pre, win_ref[:, cols], ((1,), (1,)))
        d_rows[...] = backward + d_rows[...] if n else backward
    put = puts()
    for n in range(groups):
        back_ref[n * whole : (n + 1) * whole, :] = pack(d_rows, put, n)
        returns[n].start()
    for pair in stores:
        for copy in pair:
            copy.wait()
    for copy in returns:
        copy.wait()


def rest_kernel(x_ref, g_ref, act_ref, dpre_ref, wout_ref, gin_ref, gout_ref, back_ref, result):
    n = pl.program_id(0)
    gin_ref[0] = bf16(dot(x_ref[...], dpre_ref[...], ((0,), (0,))))
    gout_ref[0] = bf16(dot(act_ref[...], g_ref[...], ((0,), (0,))))
    forward = dot(act_ref[...], wout_ref[...])

    @pl.when(n == 0)
    def _():
        result[...] = forward

    @pl.when(n > 0)
    def _():
        result[...] += forward

    @pl.when(n == pl.num_programs(0) - 1)
    def _():
        put = puts()
        half, whole = 128, 256
        for m in range(result.shape[0] // half):
            back_ref[m * whole : (m + 1) * whole, :] = pack(result, put, m)


def picked_by(key, seats):
    seat = iota((key.shape[0], seats), 1)
    return bf16(jnp.where(seat == key, 1.0, 0.0)), bf16(jnp.where(seat == key + SLOTS, 1.0, 0.0))


def out_kernel(nv_ref, key_ref, recv_hbm, conv_hbm, tie_ref, out_ref, recv_ref, conv_ref, sems):
    copies = [
        pltpu.make_async_copy(src, dst, sems.at[i])
        for i, (src, dst) in enumerate(((recv_hbm, recv_ref), (conv_hbm, conv_ref)))
    ]
    for copy in copies:
        copy.start()
    count, width = out_ref.shape
    picked = picked_by(key_ref[:, 0:1], recv_ref.shape[0])
    inside = iota((count, LANES), 0) < nv_ref[0]
    for copy in copies:
        copy.wait()
    half = width // 2
    for n in range(2):
        back = dot(picked[n], recv_ref[...])
        for i in range(half // LANES):
            c = n * (half // LANES) + i
            rows = back[:, i * LANES : (i + 1) * LANES]
            out_ref[:, c * LANES : (c + 1) * LANES] = bf16(conv_ref[c] + jnp.where(inside, rows, 0.0))


def post_kernel(
    nv_ref, row_hbm, recv_hbm, cot_hbm, inv_hbm, conv_hbm, taps_hbm, pad_hbm, tie_ref,
    dconv_ref, head_ref, tail_ref, mine_ref, other_ref, key_ref,
    row_ref, recv_ref, cot_ref, inv_ref, conv_ref, taps_ref, pad_ref,
    dhid, means, sums_ref, sems,
):
    copies = [
        pltpu.make_async_copy(src, dst, sems.at[i])
        for i, (src, dst) in enumerate(
            (
                (row_hbm, row_ref), (recv_hbm, recv_ref), (cot_hbm, cot_ref), (inv_hbm, inv_ref),
                (conv_hbm, conv_ref), (taps_hbm, taps_ref), (pad_hbm, pad_ref),
            )
        )
    ]
    for copy in copies:
        copy.start()
    count, width = cot_ref.shape
    chunks = width // LANES
    kernel = sums_ref.shape[0] - 1
    reach = (kernel - 1) // 2
    copies[0].wait()
    row = row_ref[...]
    here, there = iota((count, count), 0), iota((count, count), 1)
    col = jnp.sum(jnp.where(here == there, f32(row), 0.0), axis=1, keepdims=True).astype(jnp.int32)
    earlier = (col == row) & (there < here)
    slot = jnp.sum(jnp.where(earlier, 1.0, 0.0), axis=1, keepdims=True).astype(jnp.int32)
    key = col * PAIR + slot
    key_ref[...] = jnp.broadcast_to(key, key_ref.shape)
    picked = picked_by(key, recv_ref.shape[0])
    copies[1].wait()
    for n in range(2):
        dhid[:, n * (width // 2) : (n + 1) * (width // 2)] = dot(picked[n], recv_ref[...])
    for copy in copies[2:]:
        copy.wait()
    inv = inv_ref[...]
    means[...] = jnp.zeros_like(means)
    for c in range(chunks):
        lanes = slice(c * LANES, (c + 1) * LANES)
        normed = conv_ref[c] * inv
        d_hidden = dhid[:, lanes]
        means[...] += d_hidden * taps_ref[c, kernel : kernel + 1, :] * normed
        sums_ref[kernel : kernel + 1, lanes] = jnp.sum(d_hidden * normed, axis=0, keepdims=True)
    mean = jnp.sum(means[...], axis=-1, keepdims=True) * (1.0 / width)
    mean = jnp.broadcast_to(mean, (count, LANES))
    for c in range(chunks):
        lanes = slice(c * LANES, (c + 1) * LANES)
        d_conv = f32(cot_ref[:, lanes]) + inv * (
            dhid[:, lanes] * taps_ref[c, kernel : kernel + 1, :] - conv_ref[c] * inv * mean
        )
        dconv_ref[c] = d_conv
        head_ref[c] = d_conv[0:EDGE, :]
        tail_ref[c] = d_conv[count - EDGE :, :]
    for c in range(chunks):
        lanes = slice(c * LANES, (c + 1) * LANES)
        totals = [jnp.zeros((8, LANES), jnp.float32) for _ in range(kernel)]
        for start in range(0, count, ROWS):
            part = dconv_ref[c, start : start + ROWS, :]
            for k in range(kernel):
                at = start + k + EDGE - reach
                product = part * pad_ref[c, at : at + ROWS, :]
                totals[k] = totals[k] + jnp.sum(product.reshape(ROWS // 8, 8, LANES), axis=0)
        for k in range(kernel):
            sums_ref[k : k + 1, lanes] = jnp.sum(totals[k], axis=0, keepdims=True)
    core = nv_ref[1]
    rows = mine_ref.shape[0]
    low, high = sums_ref[0:rows, :], sums_ref[rows:, :]
    mine_ref[...] = jnp.where(core == 0, low, high)
    other_ref[...] = jnp.where(core == 0, high, low)


def back_kernel(first, nv_ref, dconv_ref, left_ref, right_ref, taps_ref, tie_ref, grad_ref, low, high):
    _, count, _ = dconv_ref.shape
    kernel = taps_ref.shape[1] - 1
    reach = (kernel - 1) // 2
    valid = nv_ref[0]
    for i in range(grad_ref.shape[1] // LANES):
        c = first + i
        lanes = slice(i * LANES, (i + 1) * LANES)
        low[i, 0:EDGE, :] = left_ref[c]
        low[i, EDGE:, :] = dconv_ref[c, 0 : ROWS + EDGE, :]
        high[i, 0 : ROWS + EDGE, :] = dconv_ref[c, count - ROWS - EDGE :, :]
        high[i, ROWS + EDGE :, :] = right_ref[c]
        for start in range(0, count, ROWS):
            if start == 0:
                window, shift, at = low, EDGE, i
            elif start == count - ROWS:
                window, shift, at = high, EDGE - start, i
            else:
                window, shift, at = dconv_ref, 0, c
            total = jnp.zeros((ROWS, LANES), jnp.float32)
            for k in range(kernel):
                begin = start + shift + reach - k
                total = total + taps_ref[c, k : k + 1, :] * window[at, begin : begin + ROWS, :]
            total = window[at, start + shift : start + shift + ROWS, :] + total
            keep = iota((ROWS, LANES), 0) + start < valid
            grad_ref[start : start + ROWS, lanes] = bf16(jnp.where(keep, total, 0.0))


def add_kernel(own_ref, one_ref, two_ref, three_ref, *refs):
    out_ref = refs[-1]
    out_ref[...] = (own_ref[...] + one_ref[...]) + (two_ref[...] + three_ref[...])


def finish_kernel(scale, nv_ref, part_ref, fellow_ref, *refs):
    pieces, (taps_ref, gain_ref, grad_ref) = refs[:-3], refs[-3:]
    core = nv_ref[1]
    rows = part_ref.shape[0]
    part, fellow = part_ref[...] * scale, fellow_ref[...] * scale
    low = jnp.where(core == 0, part, fellow)
    high = jnp.where(core == 0, fellow, part)
    taps_ref[0:rows, :] = low
    taps_ref[rows:, :] = high[0 : rows - 1, :]
    gain_ref[...] = high[rows - 1, :]
    width = pieces[0].shape[1]
    for n, piece in enumerate(pieces):
        grad_ref[:, n * width : (n + 1) * width] = piece[...]


def shifted(tail, head):
    n = lax.axis_size("tm")
    left = lax.ppermute(tail, "tm", [(i, i + 1) for i in range(n - 1)])
    right = lax.ppermute(head, "tm", [(i + 1, i) for i in range(n - 1)])
    return left, right


def local(frames, cotangent, routes, lengths, conv_weight, norm_gain, expert_in, expert_out):
    count, width = frames.shape[1:]
    kernel = conv_weight.shape[0]
    chunks = width // LANES
    devices = lax.axis_size("rec") * lax.axis_size("tm")
    hidden = expert_in.shape[2]
    rows = devices * SLOTS
    x, cot = hbm(frames[0]), hbm(cotangent[0])
    win, wout = hbm(expert_in[0]), hbm(expert_out[0])
    place = lax.axis_index("tm")
    scalars = jnp.stack([lengths[0] - place * count, place % 2])
    row = hbm(routes[0].reshape(1, count))
    conv_weight, norm_gain = hbm(conv_weight), hbm(norm_gain)
    shape = jax.ShapeDtypeStruct
    wide = shape((chunks, count, LANES), jnp.float32)
    padded = shape((chunks, count + 2 * EDGE, LANES), jnp.float32)
    lane = shape((count, LANES), jnp.float32)
    buffer = shape((2 * rows, width), jnp.bfloat16)
    half = shape(((kernel + 1) // 2, width), jnp.float32)
    conv, pad, squares, pick, grads, taps, first, last = pl.pallas_call(
        pre_kernel,
        out_shape=[
            wide, padded, lane, shape((2 * rows, count), jnp.bfloat16), buffer,
            shape((chunks, 32, LANES), jnp.float32),
            shape((EDGE, width), jnp.bfloat16),
            shape((EDGE, width), jnp.bfloat16),
        ],
        in_specs=[SMEM] + [HBM] * 5,
        out_specs=[VMEM] * 8,
        scratch_shapes=[
            pltpu.VMEM((1, count), jnp.int32),
            pltpu.VMEM((count, width), jnp.bfloat16),
            pltpu.VMEM((count, width), jnp.bfloat16),
            pltpu.VMEM((kernel, width), jnp.float32),
            pltpu.VMEM((width,), jnp.float32),
            pltpu.VMEM((count, width), jnp.bfloat16),
            pltpu.SemaphoreType.DMA((5,)),
        ],
        compiler_params=limit(20),
        cost_estimate=cost(6 * 10**9, 2 * 10**7),
        name="pre",
    )(scalars, row, x, cot, conv_weight, norm_gain)
    left, right = shifted(last, first)
    conv, pad, send, inv = pl.pallas_call(
        send_kernel,
        out_shape=[wide, padded, buffer, lane],
        in_specs=[SMEM] + [VMEM] * 8,
        out_specs=[VMEM] * 4,
        scratch_shapes=[
            pltpu.VMEM((count, width), jnp.bfloat16),
            pltpu.VMEM((count, LANES), jnp.float32),
        ],
        compiler_params=limit(20),
        cost_estimate=cost(10**9, 10**7),
        name="send",
    )(scalars, left, right, conv, pad, squares, pick, grads, taps)
    recv = lax.all_to_all(send, ("rec", "tm"), split_axis=0, concat_axis=0, tiled=True)
    wide_rows = shape((rows, hidden), jnp.bfloat16)
    these = shape((rows, width), jnp.bfloat16)
    halves = shape((2 * rows, width // 2), jnp.bfloat16)
    tiles = hidden // TILE
    back, rows_x, rows_g, act, d_pre = pl.pallas_call(
        expert_kernel,
        out_shape=[pltpu.HBM(v.shape, v.dtype) for v in (halves, these, these, wide_rows, wide_rows)],
        in_specs=[VMEM] * 3,
        out_specs=[HBM] * 5,
        scratch_shapes=[
            pltpu.VMEM((rows, width), jnp.bfloat16),
            pltpu.VMEM((rows, width), jnp.bfloat16),
            pltpu.VMEM((rows, hidden), jnp.bfloat16),
            pltpu.VMEM((rows, hidden), jnp.bfloat16),
            pltpu.VMEM((rows, width), jnp.float32),
            pltpu.VMEM((2 * rows, width // 2), jnp.bfloat16),
            pltpu.SemaphoreType.DMA((2,)),
            pltpu.SemaphoreType.DMA((rows // 128,)),
            pltpu.SemaphoreType.DMA((2, tiles)),
        ],
        compiler_params=limit(30),
        cost_estimate=cost(6 * rows * width * hidden, 2 * 10**7),
        name="experts",
    )(recv, vmem(expert_in[0]), vmem(expert_out[0]))
    home = lax.all_to_all(back, ("rec", "tm"), split_axis=0, concat_axis=0, tiled=True)
    grad_in, grad_out, back = pl.pallas_call(
        rest_kernel,
        grid=(tiles,),
        out_shape=[
            shape((1, width, hidden), jnp.bfloat16),
            shape((1, hidden, width), jnp.bfloat16),
            pltpu.HBM(halves.shape, halves.dtype),
        ],
        in_specs=[
            pl.BlockSpec((rows, width), lambda i: (0, 0)),
            pl.BlockSpec((rows, width), lambda i: (0, 0)),
            pl.BlockSpec((rows, TILE), lambda i: (0, i)),
            pl.BlockSpec((rows, TILE), lambda i: (0, i)),
            pl.BlockSpec((TILE, width), lambda i: (i, 0)),
        ],
        out_specs=[
            pl.BlockSpec((1, width, TILE), lambda i: (0, 0, i)),
            pl.BlockSpec((1, TILE, width), lambda i: (0, i, 0)),
            pl.BlockSpec((2 * rows, width // 2), lambda i: (0, 0)),
        ],
        scratch_shapes=[pltpu.VMEM((rows, width), jnp.float32)],
        compiler_params=limit(24),
        cost_estimate=cost(6 * rows * width * hidden, 2 * 10**7),
        name="weight_grads",
    )(hbm(rows_x), hbm(rows_g), hbm(act), hbm(d_pre), wout)
    home_out = lax.all_to_all(back, ("rec", "tm"), split_axis=0, concat_axis=0, tiled=True)
    edges = shape((chunks, EDGE, LANES), jnp.float32)
    d_conv, head, tail, mine, other, key = pl.pallas_call(
        post_kernel,
        out_shape=[wide, edges, edges, half, half, shape((count, LANES), jnp.int32)],
        in_specs=[SMEM] + [HBM] * 7 + [ANY],
        out_specs=[VMEM] * 6,
        scratch_shapes=[
            pltpu.VMEM((1, count), jnp.int32),
            pltpu.VMEM((2 * rows, width // 2), jnp.bfloat16),
            pltpu.VMEM((count, width), jnp.bfloat16),
            pltpu.VMEM((count, LANES), jnp.float32),
            pltpu.VMEM(wide.shape, jnp.float32),
            pltpu.VMEM((chunks, 32, LANES), jnp.float32),
            pltpu.VMEM(padded.shape, jnp.float32),
            pltpu.VMEM((count, width), jnp.float32),
            pltpu.VMEM((count, LANES), jnp.float32),
            pltpu.VMEM((kernel + 1, width), jnp.float32),
            pltpu.SemaphoreType.DMA((7,)),
        ],
        compiler_params=limit(24),
        cost_estimate=cost(10**9, 10**7),
        name="post",
    )(scalars, row, home, cot, hbm(inv), hbm(conv), hbm(taps), hbm(pad), hbm(back))
    left, right = shifted(tail, head)

    def back_part(first, tie):
        return pl.pallas_call(
            functools.partial(back_kernel, first),
            out_shape=shape((count, 2 * LANES), jnp.bfloat16),
            in_specs=[SMEM] + [VMEM] * 4 + [ANY],
            out_specs=VMEM,
            scratch_shapes=[
                pltpu.VMEM((2, ROWS + 2 * EDGE, LANES), jnp.float32),
                pltpu.VMEM((2, ROWS + 2 * EDGE, LANES), jnp.float32),
            ],
            compiler_params=limit(8),
            cost_estimate=cost(10**9, 4 * 10**6),
            name="conv_back",
        )(scalars, d_conv, left, right, taps, tie)

    def add(part, others, ties):
        return pl.pallas_call(
            add_kernel,
            out_shape=half,
            in_specs=[VMEM] * 4 + [ANY] * len(ties),
            out_specs=VMEM,
            compiler_params=limit(4),
            name="ring_add",
        )(part, *others, *ties)

    n_rec, n_tm = lax.axis_size("rec"), lax.axis_size("tm")
    swap = [(i, i ^ 1) for i in range(n_tm)]
    part = mine + lax.ppermute(other, "tm", swap)
    def out(tie):
        return pl.pallas_call(
            out_kernel,
            out_shape=shape((count, width), jnp.bfloat16),
            in_specs=[SMEM, VMEM] + [HBM] * 2 + [ANY],
            out_specs=VMEM,
            scratch_shapes=[
                pltpu.VMEM((2 * rows, width // 2), jnp.bfloat16),
                pltpu.VMEM(wide.shape, jnp.float32),
                pltpu.SemaphoreType.DMA((2,)),
            ],
            compiler_params=limit(16),
            cost_estimate=cost(10**9, 4 * 10**6),
            name="out",
        )(scalars, key, home_out, hbm(conv), tie)

    beside = (
        lambda tie: [],
        lambda tie: [back_part(0, tie), back_part(2, tie), back_part(4, tie)],
        lambda tie: [out(tie)],
    )
    done = []
    for (axis, size, step), work in zip((("tm", n_tm, 2), ("rec", n_rec, 1), ("tm", n_tm, 8)), beside):
        others = [
            lax.ppermute(part, axis, [(i, i ^ (step * flip)) for i in range(size)])
            for flip in (1, 2, 3)
        ]
        ties = work(part)
        done += ties
        part = add(part, others, ties if len(done) <= 3 else [hbm(done[3])])
    *pieces, output = done
    fellow = lax.ppermute(part, "tm", swap)
    grad_conv, grad_gain, grad_frames = pl.pallas_call(
        functools.partial(finish_kernel, 1.0 / math.sqrt(n_rec * n_tm * count)),
        out_shape=[
            shape((kernel, width), jnp.float32),
            shape((width,), jnp.float32),
            shape((count, width), jnp.bfloat16),
        ],
        in_specs=[SMEM] + [VMEM] * 5,
        out_specs=[VMEM] * 3,
        compiler_params=limit(8),
        name="finish",
    )(scalars, part, fellow, *pieces)
    return output[None], grad_frames[None], grad_conv, grad_gain, grad_in, grad_out


def solution(mesh):
    placed = (
        P("rec", "tm", None),
        P("rec", "tm", None),
        P("rec", "tm", None),
        P("rec"),
        P(),
        P(),
        P(("rec", "tm"), None, None),
        P(("rec", "tm"), None, None),
    )
    return jax.shard_map(
        local,
        mesh=mesh,
        in_specs=placed,
        out_specs=(
            P("rec", "tm", None),
            P("rec", "tm", None),
            P(),
            P(),
            P(("rec", "tm"), None, None),
            P(("rec", "tm"), None, None),
        ),
        check_vma=False,
    )
```

```python
import functools
import math

import jax
import jax.numpy as jnp
from jax import lax
from jax.experimental import pallas as pl
from jax.experimental.pallas import tpu as pltpu
from jax.sharding import PartitionSpec as P

LANES = 128
EDGE = 16
ROWS = 64
SLOTS = 4
PAIR = 2 * SLOTS
VMEM = pl.BlockSpec(memory_space=pltpu.VMEM)
SMEM = pl.BlockSpec(memory_space=pltpu.SMEM)
ANY = pl.BlockSpec(memory_space=pl.ANY)
HBM = pl.BlockSpec(memory_space=pltpu.HBM)


def f32(x):
    return x.astype(jnp.float32)


def bf16(x):
    return x.astype(jnp.bfloat16)


def dot(a, b, dims=((1,), (0,))):
    return lax.dot_general(a, b, (dims, ((), ())), preferred_element_type=jnp.float32)


def iota(shape, axis):
    return lax.broadcasted_iota(jnp.int32, shape, axis)


def limit(mebibytes):
    return pltpu.CompilerParams(vmem_limit_bytes=mebibytes * 1024 * 1024)


def vmem(x):
    return pltpu.with_memory_space_constraint(x, pltpu.VMEM)


def hbm(x):
    return pltpu.with_memory_space_constraint(x, pltpu.HBM)


def cost(flops, nbytes):
    return pl.CostEstimate(flops=flops, bytes_accessed=nbytes, transcendentals=0)


def pre_kernel(
    nv_ref, row_hbm, x_hbm, cot_hbm, w_hbm, gain_hbm,
    conv_ref, pad_ref, squares_ref, pick_ref, send_ref, taps_ref,
    row_ref, x_ref, cot_ref, w_ref, gain_ref, grads, sems,
):
    count, width = x_ref.shape
    chunks = width // LANES
    kernel = w_ref.shape[0]
    reach = (kernel - 1) // 2
    copies = [
        pltpu.make_async_copy(src, dst, sems.at[i])
        for i, (src, dst) in enumerate(
            (
                (x_hbm, x_ref), (w_hbm, w_ref), (gain_hbm, gain_ref),
                (row_hbm, row_ref), (cot_hbm, cot_ref),
            )
        )
    ]
    for copy in copies:
        copy.start()
    valid = nv_ref[0]
    inside = iota((count, LANES), 0) < valid
    squares_ref[...] = jnp.zeros_like(squares_ref)
    for copy in copies[:3]:
        copy.wait()
    for c in range(chunks):
        lanes = slice(c * LANES, (c + 1) * LANES)
        pad_ref[c, 0:EDGE, :] = jnp.zeros((EDGE, LANES), jnp.float32)
        pad_ref[c, EDGE : EDGE + count, :] = jnp.where(inside, f32(x_ref[:, lanes]), 0.0)
        pad_ref[c, EDGE + count :, :] = jnp.zeros((EDGE, LANES), jnp.float32)
        taps_ref[c, 0:kernel, :] = w_ref[:, lanes]
        taps_ref[c, kernel : kernel + 1, :] = gain_ref[lanes][None, :]

    @pl.loop(0, chunks)
    def _(c):
        for start in range(0, count, ROWS):
            total = jnp.zeros((ROWS, LANES), jnp.float32)
            for k in range(kernel):
                at = start + k + EDGE - reach
                total = total + taps_ref[c, k : k + 1, :] * pad_ref[c, at : at + ROWS, :]
            total = pad_ref[c, EDGE + start : EDGE + start + ROWS, :] + total
            conv_ref[c, start : start + ROWS, :] = total
            if 0 < start < count - ROWS:
                squares_ref[start : start + ROWS, :] += total * total
            else:
                low = EDGE if start == 0 else 0
                high = ROWS if start == 0 else ROWS - EDGE
                inner = total[low:high, :]
                squares_ref[start + low : start + high, :] += inner * inner

    for copy in copies[3:]:
        copy.wait()
    row = row_ref[...]
    experts = send_ref.shape[0] // PAIR
    named = jnp.where(iota((experts, count), 0) == row, 1.0, 0.0)
    before = bf16(jnp.where(iota((count, count), 0) < iota((count, count), 1), 1.0, 0.0))
    slot = jnp.sum(named * dot(bf16(named), before), axis=0, keepdims=True)
    key = row * PAIR + slot.astype(jnp.int32)
    for c in range(chunks):
        lanes = slice(c * LANES, (c + 1) * LANES)
        grads[:, lanes] = bf16(jnp.where(inside, f32(cot_ref[:, lanes]), 0.0))
    block = 256
    for start in range(0, send_ref.shape[0], block):
        seat = iota((block, count), 0) + start
        pick_ref[start : start + block, :] = bf16(jnp.where(seat == key, 1.0, 0.0))
        pick = bf16(jnp.where(seat == key + SLOTS, 1.0, 0.0))
        send_ref[start : start + block, :] = bf16(dot(pick, grads[...]))


def send_kernel(
    nv_ref, left_ref, right_ref, conv_in, pad_in, squares_ref, pick_ref, grads_ref, taps_ref,
    conv_ref, pad_ref, send_ref, inv_ref,
    rows, squares,
):
    chunks, count, _ = conv_in.shape
    width = chunks * LANES
    kernel = taps_ref.shape[1] - 1
    reach = (kernel - 1) // 2
    valid = nv_ref[0]
    edge = iota((EDGE, LANES), 0)
    squares[...] = squares_ref[...]
    for c in range(chunks):
        lanes = slice(c * LANES, (c + 1) * LANES)
        pad_ref[c, 0:EDGE, :] = jnp.where(edge - EDGE < valid, f32(left_ref[:, lanes]), 0.0)
        pad_ref[c, EDGE : EDGE + count, :] = pad_in[c, EDGE : EDGE + count, :]
        pad_ref[c, EDGE + count :, :] = jnp.where(edge + count < valid, f32(right_ref[:, lanes]), 0.0)
        conv_ref[c, EDGE : count - EDGE, :] = conv_in[c, EDGE : count - EDGE, :]
        for start in (0, count - EDGE):
            total = jnp.zeros((EDGE, LANES), jnp.float32)
            for k in range(kernel):
                at = start + k + EDGE - reach
                total = total + taps_ref[c, k : k + 1, :] * pad_ref[c, at : at + EDGE, :]
            total = pad_ref[c, EDGE + start : EDGE + start + EDGE, :] + total
            conv_ref[c, start : start + EDGE, :] = total
            squares[start : start + EDGE, :] += total * total
    inv = lax.rsqrt(jnp.sum(squares[...], axis=-1, keepdims=True) * (1.0 / width) + 1e-05)
    inv = jnp.broadcast_to(inv, (count, LANES))
    inv_ref[...] = inv
    for c in range(chunks):
        lanes = slice(c * LANES, (c + 1) * LANES)
        rows[:, lanes] = bf16(conv_ref[c] * inv * taps_ref[c, kernel : kernel + 1, :])
    block = 256
    for start in range(0, send_ref.shape[0], block):
        part = slice(start, start + block)
        send_ref[part, :] = bf16(dot(pick_ref[part, :], rows[...]) + f32(grads_ref[part, :]))


def picks():
    half, whole = 128, 256
    i, r = iota((half, whole), 0), iota((half, whole), 1)
    place = (i // SLOTS) * PAIR + i % SLOTS
    return bf16(jnp.where(r == place, 1.0, 0.0)), bf16(jnp.where(r == place + SLOTS, 1.0, 0.0))


def unpack(recv_ref, x_ref, g_ref):
    pick_x, pick_g = picks()
    half, whole = pick_x.shape
    for n in range(x_ref.shape[0] // half):
        part = recv_ref[n * whole : (n + 1) * whole, :]
        x_ref[n * half : (n + 1) * half, :] = bf16(dot(pick_x, part))
        g_ref[n * half : (n + 1) * half, :] = bf16(dot(pick_g, part))


def pack(rows, put, n):
    half = put[0].shape[1]
    part = bf16(rows[n * half : (n + 1) * half, :])
    cut = part.shape[1] // 2
    return bf16(dot(put[0], part[:, :cut]) + dot(put[1], part[:, cut:]))


def puts():
    half, whole = 128, 256
    q, j = iota((whole, half), 0), iota((whole, half), 1)
    home = (j // SLOTS) * PAIR + j % SLOTS
    return bf16(jnp.where(q == home, 1.0, 0.0)), bf16(jnp.where(q == home + SLOTS, 1.0, 0.0))


TILE = 768


def expert_kernel(
    recv_ref, win_ref, wout_ref,
    back_hbm, x_hbm, g_hbm, act_hbm, dpre_hbm,
    x_ref, g_ref, act_ref, dpre_ref, d_rows, back_ref, row_sems, back_sems, out_sems,
):
    rows = x_ref.shape[0]
    hidden = win_ref.shape[1]
    tiles = hidden // TILE
    half, whole = 128, 256
    groups = rows // half
    returns, stores = [], []
    for n in range(groups):
        part = pl.ds(n * whole, whole)
        returns.append(pltpu.make_async_copy(back_ref.at[part, :], back_hbm.at[part, :], back_sems.at[n]))
    for n in range(tiles):
        cols = pl.ds(n * TILE, TILE)
        stores.append((
            pltpu.make_async_copy(act_ref.at[:, cols], act_hbm.at[:, cols], out_sems.at[0, n]),
            pltpu.make_async_copy(dpre_ref.at[:, cols], dpre_hbm.at[:, cols], out_sems.at[1, n]),
        ))
    unpack(recv_ref, x_ref, g_ref)
    stores.append((
        pltpu.make_async_copy(x_ref, x_hbm, row_sems.at[0]),
        pltpu.make_async_copy(g_ref, g_hbm, row_sems.at[1]),
    ))
    for copy in stores[tiles]:
        copy.start()

    def front(n):
        cols = slice(n * TILE, (n + 1) * TILE)
        return (
            dot(x_ref[...], win_ref[:, cols]),
            dot(g_ref[...], wout_ref[cols, :], ((1,), (1,))),
        )

    ready = front(0)
    for n in range(tiles):
        cols = slice(n * TILE, (n + 1) * TILE)
        pre, d_act = ready
        if n + 1 < tiles:
            ready = front(n + 1)
        gate = 0.5 * jnp.tanh(0.5 * pre) + 0.5
        value = pre * gate
        d_pre = bf16(d_act * (gate + value * (1.0 - gate)))
        act_ref[:, cols] = bf16(value)
        dpre_ref[:, cols] = d_pre
        for copy in stores[n]:
            copy.start()
        backward = dot(d_pre, win_ref[:, cols], ((1,), (1,)))
        d_rows[...] = backward + d_rows[...] if n else backward
    put = puts()
    for n in range(groups):
        back_ref[n * whole : (n + 1) * whole, :] = pack(d_rows, put, n)
        returns[n].start()
    for pair in stores:
        for copy in pair:
            copy.wait()
    for copy in returns:
        copy.wait()


def rest_kernel(x_ref, g_ref, act_ref, dpre_ref, wout_ref, gin_ref, gout_ref, back_ref, result):
    n = pl.program_id(0)
    gin_ref[0] = bf16(dot(x_ref[...], dpre_ref[...], ((0,), (0,))))
    gout_ref[0] = bf16(dot(act_ref[...], g_ref[...], ((0,), (0,))))
    forward = dot(act_ref[...], wout_ref[...])

    @pl.when(n == 0)
    def _():
        result[...] = forward

    @pl.when(n > 0)
    def _():
        result[...] += forward

    @pl.when(n == pl.num_programs(0) - 1)
    def _():
        put = puts()
        half, whole = 128, 256
        for m in range(result.shape[0] // half):
            back_ref[m * whole : (m + 1) * whole, :] = pack(result, put, m)


def picked_by(key, seats):
    seat = iota((key.shape[0], seats), 1)
    return bf16(jnp.where(seat == key, 1.0, 0.0)), bf16(jnp.where(seat == key + SLOTS, 1.0, 0.0))


def out_kernel(nv_ref, key_ref, recv_hbm, conv_hbm, tie_ref, out_ref, recv_ref, conv_ref, sems):
    copies = [
        pltpu.make_async_copy(src, dst, sems.at[i])
        for i, (src, dst) in enumerate(((recv_hbm, recv_ref), (conv_hbm, conv_ref)))
    ]
    for copy in copies:
        copy.start()
    count, width = out_ref.shape
    picked = picked_by(key_ref[:, 0:1], recv_ref.shape[0])
    inside = iota((count, LANES), 0) < nv_ref[0]
    for copy in copies:
        copy.wait()
    half = width // 2
    for n in range(2):
        back = dot(picked[n], recv_ref[...])
        for i in range(half // LANES):
            c = n * (half // LANES) + i
            rows = back[:, i * LANES : (i + 1) * LANES]
            out_ref[:, c * LANES : (c + 1) * LANES] = bf16(conv_ref[c] + jnp.where(inside, rows, 0.0))


def post_kernel(
    nv_ref, row_hbm, recv_hbm, cot_hbm, inv_hbm, conv_hbm, taps_hbm, pad_hbm, tie_ref,
    dconv_ref, head_ref, tail_ref, mine_ref, other_ref, key_ref,
    row_ref, recv_ref, cot_ref, inv_ref, conv_ref, taps_ref, pad_ref,
    dhid, means, sums_ref, sems,
):
    copies = [
        pltpu.make_async_copy(src, dst, sems.at[i])
        for i, (src, dst) in enumerate(
            (
                (row_hbm, row_ref), (recv_hbm, recv_ref), (cot_hbm, cot_ref), (inv_hbm, inv_ref),
                (conv_hbm, conv_ref), (taps_hbm, taps_ref), (pad_hbm, pad_ref),
            )
        )
    ]
    for copy in copies:
        copy.start()
    count, width = cot_ref.shape
    chunks = width // LANES
    kernel = sums_ref.shape[0] - 1
    reach = (kernel - 1) // 2
    copies[0].wait()
    row = row_ref[...]
    here, there = iota((count, count), 0), iota((count, count), 1)
    col = jnp.sum(jnp.where(here == there, f32(row), 0.0), axis=1, keepdims=True).astype(jnp.int32)
    earlier = (col == row) & (there < here)
    slot = jnp.sum(jnp.where(earlier, 1.0, 0.0), axis=1, keepdims=True).astype(jnp.int32)
    key = col * PAIR + slot
    key_ref[...] = jnp.broadcast_to(key, key_ref.shape)
    picked = picked_by(key, recv_ref.shape[0])
    copies[1].wait()
    for n in range(2):
        dhid[:, n * (width // 2) : (n + 1) * (width // 2)] = dot(picked[n], recv_ref[...])
    for copy in copies[2:]:
        copy.wait()
    inv = inv_ref[...]
    means[...] = jnp.zeros_like(means)
    for c in range(chunks):
        lanes = slice(c * LANES, (c + 1) * LANES)
        normed = conv_ref[c] * inv
        d_hidden = dhid[:, lanes]
        means[...] += d_hidden * taps_ref[c, kernel : kernel + 1, :] * normed
        sums_ref[kernel : kernel + 1, lanes] = jnp.sum(d_hidden * normed, axis=0, keepdims=True)
    mean = jnp.sum(means[...], axis=-1, keepdims=True) * (1.0 / width)
    mean = jnp.broadcast_to(mean, (count, LANES))
    for c in range(chunks):
        lanes = slice(c * LANES, (c + 1) * LANES)
        d_conv = f32(cot_ref[:, lanes]) + inv * (
            dhid[:, lanes] * taps_ref[c, kernel : kernel + 1, :] - conv_ref[c] * inv * mean
        )
        dconv_ref[c] = d_conv
        head_ref[c] = d_conv[0:EDGE, :]
        tail_ref[c] = d_conv[count - EDGE :, :]
    for c in range(chunks):
        lanes = slice(c * LANES, (c + 1) * LANES)
        totals = [jnp.zeros((8, LANES), jnp.float32) for _ in range(kernel)]
        for start in range(0, count, ROWS):
            part = dconv_ref[c, start : start + ROWS, :]
            for k in range(kernel):
                at = start + k + EDGE - reach
                product = part * pad_ref[c, at : at + ROWS, :]
                totals[k] = totals[k] + jnp.sum(product.reshape(ROWS // 8, 8, LANES), axis=0)
        for k in range(kernel):
            sums_ref[k : k + 1, lanes] = jnp.sum(totals[k], axis=0, keepdims=True)
    core = nv_ref[1]
    rows = mine_ref.shape[0]
    low, high = sums_ref[0:rows, :], sums_ref[rows:, :]
    mine_ref[...] = jnp.where(core == 0, low, high)
    other_ref[...] = jnp.where(core == 0, high, low)


def back_kernel(first, nv_ref, dconv_ref, left_ref, right_ref, taps_ref, tie_ref, grad_ref, low, high):
    _, count, _ = dconv_ref.shape
    kernel = taps_ref.shape[1] - 1
    reach = (kernel - 1) // 2
    valid = nv_ref[0]
    for i in range(grad_ref.shape[1] // LANES):
        c = first + i
        lanes = slice(i * LANES, (i + 1) * LANES)
        low[i, 0:EDGE, :] = left_ref[c]
        low[i, EDGE:, :] = dconv_ref[c, 0 : ROWS + EDGE, :]
        high[i, 0 : ROWS + EDGE, :] = dconv_ref[c, count - ROWS - EDGE :, :]
        high[i, ROWS + EDGE :, :] = right_ref[c]
        for start in range(0, count, ROWS):
            if start == 0:
                window, shift, at = low, EDGE, i
            elif start == count - ROWS:
                window, shift, at = high, EDGE - start, i
            else:
                window, shift, at = dconv_ref, 0, c
            total = jnp.zeros((ROWS, LANES), jnp.float32)
            for k in range(kernel):
                begin = start + shift + reach - k
                total = total + taps_ref[c, k : k + 1, :] * window[at, begin : begin + ROWS, :]
            total = window[at, start + shift : start + shift + ROWS, :] + total
            keep = iota((ROWS, LANES), 0) + start < valid
            grad_ref[start : start + ROWS, lanes] = bf16(jnp.where(keep, total, 0.0))


def add_kernel(own_ref, one_ref, two_ref, three_ref, *refs):
    out_ref = refs[-1]
    out_ref[...] = (own_ref[...] + one_ref[...]) + (two_ref[...] + three_ref[...])


def finish_kernel(scale, nv_ref, part_ref, fellow_ref, *refs):
    pieces, (taps_ref, gain_ref, grad_ref) = refs[:-3], refs[-3:]
    core = nv_ref[1]
    rows = part_ref.shape[0]
    part, fellow = part_ref[...] * scale, fellow_ref[...] * scale
    low = jnp.where(core == 0, part, fellow)
    high = jnp.where(core == 0, fellow, part)
    taps_ref[0:rows, :] = low
    taps_ref[rows:, :] = high[0 : rows - 1, :]
    gain_ref[...] = high[rows - 1, :]
    width = pieces[0].shape[1]
    for n, piece in enumerate(pieces):
        grad_ref[:, n * width : (n + 1) * width] = piece[...]


def shifted(tail, head):
    n = lax.axis_size("tm")
    left = lax.ppermute(tail, "tm", [(i, i + 1) for i in range(n - 1)])
    right = lax.ppermute(head, "tm", [(i + 1, i) for i in range(n - 1)])
    return left, right


def local(frames, cotangent, routes, lengths, conv_weight, norm_gain, expert_in, expert_out):
    count, width = frames.shape[1:]
    kernel = conv_weight.shape[0]
    chunks = width // LANES
    devices = lax.axis_size("rec") * lax.axis_size("tm")
    hidden = expert_in.shape[2]
    rows = devices * SLOTS
    x, cot = hbm(frames[0]), hbm(cotangent[0])
    win, wout = hbm(expert_in[0]), hbm(expert_out[0])
    place = lax.axis_index("tm")
    scalars = jnp.stack([lengths[0] - place * count, place % 2])
    row = hbm(routes[0].reshape(1, count))
    conv_weight, norm_gain = hbm(conv_weight), hbm(norm_gain)
    shape = jax.ShapeDtypeStruct
    wide = shape((chunks, count, LANES), jnp.float32)
    padded = shape((chunks, count + 2 * EDGE, LANES), jnp.float32)
    lane = shape((count, LANES), jnp.float32)
    buffer = shape((2 * rows, width), jnp.bfloat16)
    half = shape(((kernel + 1) // 2, width), jnp.float32)
    left, right = shifted(frames[0, count - EDGE :], frames[0, :EDGE])
    conv, pad, squares, pick, grads, taps = pl.pallas_call(
        pre_kernel,
        out_shape=[
            wide, padded, lane, shape((2 * rows, count), jnp.bfloat16), buffer,
            shape((chunks, 32, LANES), jnp.float32),
        ],
        in_specs=[SMEM] + [HBM] * 5,
        out_specs=[VMEM] * 6,
        scratch_shapes=[
            pltpu.VMEM((1, count), jnp.int32),
            pltpu.VMEM((count, width), jnp.bfloat16),
            pltpu.VMEM((count, width), jnp.bfloat16),
            pltpu.VMEM((kernel, width), jnp.float32),
            pltpu.VMEM((width,), jnp.float32),
            pltpu.VMEM((count, width), jnp.bfloat16),
            pltpu.SemaphoreType.DMA((5,)),
        ],
        compiler_params=limit(20),
        cost_estimate=cost(6 * 10**9, 2 * 10**7),
        name="pre",
    )(scalars, row, x, cot, conv_weight, norm_gain)
    conv, pad, send, inv = pl.pallas_call(
        send_kernel,
        out_shape=[wide, padded, buffer, lane],
        in_specs=[SMEM] + [VMEM] * 8,
        out_specs=[VMEM] * 4,
        scratch_shapes=[
            pltpu.VMEM((count, width), jnp.bfloat16),
            pltpu.VMEM((count, LANES), jnp.float32),
        ],
        compiler_params=limit(20),
        cost_estimate=cost(10**9, 10**7),
        name="send",
    )(scalars, left, right, conv, pad, squares, pick, grads, taps)
    recv = lax.all_to_all(send, ("rec", "tm"), split_axis=0, concat_axis=0, tiled=True)
    wide_rows = shape((rows, hidden), jnp.bfloat16)
    these = shape((rows, width), jnp.bfloat16)
    halves = shape((2 * rows, width // 2), jnp.bfloat16)
    tiles = hidden // TILE
    back, rows_x, rows_g, act, d_pre = pl.pallas_call(
        expert_kernel,
        out_shape=[pltpu.HBM(v.shape, v.dtype) for v in (halves, these, these, wide_rows, wide_rows)],
        in_specs=[VMEM] * 3,
        out_specs=[HBM] * 5,
        scratch_shapes=[
            pltpu.VMEM((rows, width), jnp.bfloat16),
            pltpu.VMEM((rows, width), jnp.bfloat16),
            pltpu.VMEM((rows, hidden), jnp.bfloat16),
            pltpu.VMEM((rows, hidden), jnp.bfloat16),
            pltpu.VMEM((rows, width), jnp.float32),
            pltpu.VMEM((2 * rows, width // 2), jnp.bfloat16),
            pltpu.SemaphoreType.DMA((2,)),
            pltpu.SemaphoreType.DMA((rows // 128,)),
            pltpu.SemaphoreType.DMA((2, tiles)),
        ],
        compiler_params=limit(30),
        cost_estimate=cost(6 * rows * width * hidden, 2 * 10**7),
        name="experts",
    )(recv, vmem(expert_in[0]), vmem(expert_out[0]))
    home = lax.all_to_all(back, ("rec", "tm"), split_axis=0, concat_axis=0, tiled=True)
    grad_in, grad_out, back = pl.pallas_call(
        rest_kernel,
        grid=(tiles,),
        out_shape=[
            shape((1, width, hidden), jnp.bfloat16),
            shape((1, hidden, width), jnp.bfloat16),
            pltpu.HBM(halves.shape, halves.dtype),
        ],
        in_specs=[
            pl.BlockSpec((rows, width), lambda i: (0, 0)),
            pl.BlockSpec((rows, width), lambda i: (0, 0)),
            pl.BlockSpec((rows, TILE), lambda i: (0, i)),
            pl.BlockSpec((rows, TILE), lambda i: (0, i)),
            pl.BlockSpec((TILE, width), lambda i: (i, 0)),
        ],
        out_specs=[
            pl.BlockSpec((1, width, TILE), lambda i: (0, 0, i)),
            pl.BlockSpec((1, TILE, width), lambda i: (0, i, 0)),
            pl.BlockSpec((2 * rows, width // 2), lambda i: (0, 0)),
        ],
        scratch_shapes=[pltpu.VMEM((rows, width), jnp.float32)],
        compiler_params=limit(24),
        cost_estimate=cost(6 * rows * width * hidden, 2 * 10**7),
        name="weight_grads",
    )(hbm(rows_x), hbm(rows_g), hbm(act), hbm(d_pre), wout)
    home_out = lax.all_to_all(back, ("rec", "tm"), split_axis=0, concat_axis=0, tiled=True)
    edges = shape((chunks, EDGE, LANES), jnp.float32)
    d_conv, head, tail, mine, other, key = pl.pallas_call(
        post_kernel,
        out_shape=[wide, edges, edges, half, half, shape((count, LANES), jnp.int32)],
        in_specs=[SMEM] + [HBM] * 7 + [ANY],
        out_specs=[VMEM] * 6,
        scratch_shapes=[
            pltpu.VMEM((1, count), jnp.int32),
            pltpu.VMEM((2 * rows, width // 2), jnp.bfloat16),
            pltpu.VMEM((count, width), jnp.bfloat16),
            pltpu.VMEM((count, LANES), jnp.float32),
            pltpu.VMEM(wide.shape, jnp.float32),
            pltpu.VMEM((chunks, 32, LANES), jnp.float32),
            pltpu.VMEM(padded.shape, jnp.float32),
            pltpu.VMEM((count, width), jnp.float32),
            pltpu.VMEM((count, LANES), jnp.float32),
            pltpu.VMEM((kernel + 1, width), jnp.float32),
            pltpu.SemaphoreType.DMA((7,)),
        ],
        compiler_params=limit(24),
        cost_estimate=cost(10**9, 10**7),
        name="post",
    )(scalars, row, home, cot, hbm(inv), hbm(conv), hbm(taps), hbm(pad), hbm(back))
    left, right = shifted(tail, head)

    def back_part(first, tie):
        return pl.pallas_call(
            functools.partial(back_kernel, first),
            out_shape=shape((count, 2 * LANES), jnp.bfloat16),
            in_specs=[SMEM] + [VMEM] * 4 + [ANY],
            out_specs=VMEM,
            scratch_shapes=[
                pltpu.VMEM((2, ROWS + 2 * EDGE, LANES), jnp.float32),
                pltpu.VMEM((2, ROWS + 2 * EDGE, LANES), jnp.float32),
            ],
            compiler_params=limit(8),
            cost_estimate=cost(10**9, 4 * 10**6),
            name="conv_back",
        )(scalars, d_conv, left, right, taps, tie)

    def add(part, others, ties):
        return pl.pallas_call(
            add_kernel,
            out_shape=half,
            in_specs=[VMEM] * 4 + [ANY] * len(ties),
            out_specs=VMEM,
            compiler_params=limit(4),
            name="ring_add",
        )(part, *others, *ties)

    n_rec, n_tm = lax.axis_size("rec"), lax.axis_size("tm")
    swap = [(i, i ^ 1) for i in range(n_tm)]
    part = mine + lax.ppermute(other, "tm", swap)
    def out(tie):
        return pl.pallas_call(
            out_kernel,
            out_shape=shape((count, width), jnp.bfloat16),
            in_specs=[SMEM, VMEM] + [HBM] * 2 + [ANY],
            out_specs=VMEM,
            scratch_shapes=[
                pltpu.VMEM((2 * rows, width // 2), jnp.bfloat16),
                pltpu.VMEM(wide.shape, jnp.float32),
                pltpu.SemaphoreType.DMA((2,)),
            ],
            compiler_params=limit(16),
            cost_estimate=cost(10**9, 4 * 10**6),
            name="out",
        )(scalars, key, home_out, hbm(conv), tie)

    beside = (
        lambda tie: [],
        lambda tie: [back_part(0, tie), back_part(2, tie), back_part(4, tie)],
        lambda tie: [out(tie)],
    )
    done = []
    for (axis, size, step), work in zip((("tm", n_tm, 2), ("rec", n_rec, 1), ("tm", n_tm, 8)), beside):
        others = [
            lax.ppermute(part, axis, [(i, i ^ (step * flip)) for i in range(size)])
            for flip in (1, 2, 3)
        ]
        ties = work(part)
        done += ties
        part = add(part, others, ties if len(done) <= 3 else [hbm(done[3])])
    *pieces, output = done
    fellow = lax.ppermute(part, "tm", swap)
    grad_conv, grad_gain, grad_frames = pl.pallas_call(
        functools.partial(finish_kernel, 1.0 / math.sqrt(n_rec * n_tm * count)),
        out_shape=[
            shape((kernel, width), jnp.float32),
            shape((width,), jnp.float32),
            shape((count, width), jnp.bfloat16),
        ],
        in_specs=[SMEM] + [VMEM] * 5,
        out_specs=[VMEM] * 3,
        compiler_params=limit(8),
        name="finish",
    )(scalars, part, fellow, *pieces)
    return output[None], grad_frames[None], grad_conv, grad_gain, grad_in, grad_out


def solution(mesh):
    placed = (
        P("rec", "tm", None),
        P("rec", "tm", None),
        P("rec", "tm", None),
        P("rec"),
        P(),
        P(),
        P(("rec", "tm"), None, None),
        P(("rec", "tm"), None, None),
    )
    return jax.shard_map(
        local,
        mesh=mesh,
        in_specs=placed,
        out_specs=(
            P("rec", "tm", None),
            P("rec", "tm", None),
            P(),
            P(),
            P(("rec", "tm"), None, None),
            P(("rec", "tm"), None, None),
        ),
        check_vma=False,
    )
```
